256 devices in a mesh: harm: 4 (over z_hi, core), space: 16 (over x, y), samp: 4 (over z_lo).
Axes of the slice: x: 4, y: 4, z: 8 (z_hi: 2, z_lo: 4; z = z_hi * 4 + z_lo), core: 2. Of those that a mesh axis runs over, the one named last changes fastest.
Arguments:
- coeffs: bfloat16 [32, 32768], P(('harm', 'samp'), 'space'), may hold values from -1.5 to 1.5
- curl_tiles: bfloat16 [256, 4, 128, 384], P('space'), may hold values from -0.25 to 0.25
- pattern: int32 [256, 4], P('space'), may hold values from 0 to 17, as said below
- region_ids: int32 [256], P('space'), may hold values from 0 to 3
- material_law: float32 [3, 4], replicated, may hold values from 0.3 to 3
- source: float32 [32, 32768], P(('harm', 'samp'), 'space'), may hold values from -6 to 6
Outputs:
- residual: float32 [32, 32768], P(('harm', 'samp'), 'space')
The draws below stay inside these ranges and needn't reach their ends.
Inputs may be any that keep to these rules, and one draw needn't show every extreme that they name: `pattern`: entries index a space shard's window of 18 edge tiles: 0 is the last tile of the previous shard, 17 the first of the next, cyclically over the sector; the first entry of every row is the element tile's own position in its shard plus one.
All inputs are finite; a program needn't handle non-finite values.
Results may differ from the reference program's by a relative error of at most 0.0015.
Values may be sent and summed in bfloat16 or wider, within the bound.
A program may use at most 64 MiB of HBM per device.

```python
import math
import jax
import jax.numpy as jnp
from jax import lax

SAMPLES = 64
TILE = 128
LINKS = 4
REGIONS = 4
TILES = 16
PARTS_SIZE = 32
ELEM_TILES = 256
EDGES = 32768


def draw_pattern(key, part):
    owners = jnp.arange(ELEM_TILES, dtype=jnp.int32) % TILES
    nearby = owners[:, None] + jax.random.randint(jax.random.fold_in(key, 11), (ELEM_TILES, 2), 0, 3).astype(jnp.int32)
    distant = jax.random.randint(jax.random.fold_in(key, 23), (ELEM_TILES, LINKS - 3), 0, TILES + 2).astype(jnp.int32)
    return jnp.concatenate([owners[:, None] + 1, nearby, distant], axis=1).astype(jnp.int32)


def touch_ends(values, key, smallest, high):
    spot = [jax.random.randint(jax.random.fold_in(key, axis), (), 0, length) for axis, length in enumerate(values.shape)]
    widest = values.shape.index(max(values.shape))
    neighbour = spot[:widest] + [(spot[widest] + 1) % values.shape[widest]] + spot[widest + 1:]
    return values.at[tuple(spot)].set(smallest).at[tuple(neighbour)].set(high)


def shard_levels(rng, extent, shards, least, top_value):
    level = 1.0
    for axis_at, parts in shards:
        heights = jax.random.uniform(jax.random.fold_in(jax.random.fold_in(rng, 6), axis_at), (parts,), jnp.float32, least / len(shards), top_value / len(shards))
        level = level * jnp.repeat(jnp.exp(heights), extent[axis_at] // parts).reshape((-1,) + (1,) * (len(extent) - 1 - axis_at))
    return level


def noise(own_key, extent, width, bound, cuts=(), kind=jnp.bfloat16):
    level = shard_levels(own_key, extent, cuts, -0.22, 0.18) if cuts else 1.0
    entries = jax.random.normal(own_key, extent, jnp.float32) * width * level
    return jnp.minimum(jnp.maximum(entries, -bound), bound).astype(kind)


def setup_inputs(seed: int = 0) -> dict:
    key_list = jax.random.split(jax.random.key(seed), 7)
    coeffs = noise(key_list[0], (PARTS_SIZE, EDGES), 0.25, 1.5, ((0, 16), (1, 16)))
    curl_tiles = noise(key_list[1], (ELEM_TILES, LINKS, TILE, 3 * TILE), (LINKS * TILE) ** -0.5, 0.25, ((0, 16),))
    pattern = draw_pattern(jax.random.fold_in(key_list[6], 71), 0)
    region_ids = touch_ends(jax.random.randint(key_list[3], (ELEM_TILES,), 0, REGIONS), jax.random.fold_in(key_list[3], 1), 0, REGIONS - 1).astype(jnp.int32)
    material_law = jnp.clip(jnp.exp(jax.random.uniform(key_list[4], (3, REGIONS), jnp.float32, math.log(0.3), math.log(3.0))), 0.3, 3.0)
    source = noise(key_list[5], (PARTS_SIZE, EDGES), 1.0, 6.0, ((0, 16), (1, 16)), jnp.float32)
    return dict(coeffs=coeffs, curl_tiles=curl_tiles, pattern=pattern, region_ids=region_ids, material_law=material_law, source=source)


def transform_table():
    sample_ids = jnp.arange(SAMPLES, dtype=jnp.int32)[:, None]
    part_ids = jnp.arange(PARTS_SIZE, dtype=jnp.int32)[None, :]
    orders = 2 * (part_ids // 2) + 1
    phase = ((orders * sample_ids) % SAMPLES).astype(jnp.float32) * (2.0 * math.pi / SAMPLES)
    return jnp.where(part_ids % 2 == 0, jnp.cos(phase), jnp.sin(phase))


def reference(coeffs, curl_tiles, pattern, region_ids, material_law, source):
    transform = transform_table()
    shard_of = jnp.arange(ELEM_TILES, dtype=jnp.int32) // TILES
    edge_index = ((shard_of[:, None] * TILES + pattern - 1) % ELEM_TILES).astype(jnp.int32)
    coeff_tiles = coeffs.reshape(PARTS_SIZE, ELEM_TILES, TILE)
    picked = coeff_tiles[:, edge_index.reshape(-1)].reshape(PARTS_SIZE, ELEM_TILES, LINKS, TILE)
    curl_wide = curl_tiles.astype(jnp.float32)
    flux_rows = jnp.einsum("pgki,gkij->pgj", picked.astype(jnp.float32), curl_wide, precision=lax.Precision.HIGHEST)
    flux_rows = flux_rows.reshape(PARTS_SIZE, ELEM_TILES * 3 * TILE)
    density = jnp.dot(transform, flux_rows, precision=lax.Precision.HIGHEST, preferred_element_type=jnp.float32)
    density = density.reshape(SAMPLES, ELEM_TILES, 3, TILE)
    magnitude = jnp.sum(density * density, axis=2)
    region_hits = (region_ids[:, None] == jnp.arange(REGIONS, dtype=jnp.int32)[None, :]).astype(jnp.float32)
    region_law = jnp.dot(region_hits, material_law.T, precision=lax.Precision.HIGHEST, preferred_element_type=jnp.float32)
    base_value = region_law[:, 0][None, :, None]
    knee_value = region_law[:, 1][None, :, None]
    rise_value = region_law[:, 2][None, :, None]
    reluct = base_value + rise_value * magnitude / (magnitude + knee_value)
    field = (reluct[:, :, None, :] * density).reshape(SAMPLES, ELEM_TILES * 3 * TILE)
    harm_field = (2.0 / SAMPLES) * jnp.dot(transform.T, field, precision=lax.Precision.HIGHEST, preferred_element_type=jnp.float32)
    field_half = harm_field.astype(jnp.bfloat16).reshape(PARTS_SIZE, ELEM_TILES, 3 * TILE)
    contrib = jnp.einsum("pgj,gkij->pgki", field_half.astype(jnp.float32), curl_wide, precision=lax.Precision.HIGHEST)
    accumulated = jnp.zeros((PARTS_SIZE, ELEM_TILES, TILE), jnp.float32)
    accumulated = accumulated.at[:, edge_index.reshape(-1)].add(contrib.reshape(PARTS_SIZE, ELEM_TILES * LINKS, TILE))
    return accumulated.reshape(PARTS_SIZE, EDGES) - source
```

```python
import math

import jax
import jax.numpy as jnp
import ml_dtypes
import numpy as np
from jax import lax
from jax.experimental import pallas as pl
from jax.experimental.pallas import tpu as pltpu
from jax.sharding import PartitionSpec as P

SAMPLES = 64
HALF = SAMPLES // 2
PARTS = 32
GROUP = 16
SPACE = 16
TILES = 16
LINKS = 4
TILE = 128
COMP = 3 * TILE
MESH = pl.DeviceIdType.MESH
F32, BF16 = jnp.float32, jnp.bfloat16


def two_pieces(table):
    high = table.astype(ml_dtypes.bfloat16)
    low = (table - high.astype(np.float64)).astype(ml_dtypes.bfloat16)
    return high, low


def tables():
    t = np.arange(HALF)[:, None]
    q = np.arange(PARTS)[None, :]
    phase = ((2 * (q // 2) + 1) * t % SAMPLES) * (2.0 * math.pi / SAMPLES)
    transform = np.where(q % 2 == 0, np.cos(phase), np.sin(phase))
    main = np.zeros((LINKS, HALF, GROUP, LINKS, 2))
    for k in range(LINKS):
        main[k, :, :, k, :] = transform.reshape(HALF, GROUP, 2)
    forward = np.concatenate(
        [
            main.reshape(LINKS * HALF, GROUP * LINKS * 2),
            np.tile(transform, (LINKS, 2)),
            np.zeros((LINKS * HALF, 64)),
        ],
        axis=1,
    )
    back = (4.0 / SAMPLES) * transform.reshape(HALF, GROUP, 2).transpose(2, 1, 0).reshape(PARTS, HALF)
    back_high, back_low = two_pieces(back)
    back_row = np.zeros((PARTS, 256), ml_dtypes.bfloat16)
    back_row[:, : 3 * HALF] = np.concatenate([back_high, back_low, back_high], axis=1)
    return np.concatenate([*two_pieces(forward), back_row], axis=0)


def split(value):
    high = value.astype(BF16)
    return high, (value - high.astype(F32)).astype(BF16)


def kernel(
    coef_hbm, curl_hbm, pat_hbm, reg_hbm, law_hbm, tab_hbm, out_ref,
    coef, curl, pat, reg, law, tab, picks, got, low_got, high_got, sums,
    flow, flow_got, edge_flow, low_flow, high_flow, local_sem, send_sem, recv_sem,
):
    harm, space, samp = lax.axis_index("harm"), lax.axis_index("space"), lax.axis_index("samp")
    rank = harm * 4 + samp

    def at(group, other):
        return (other // 4, group, lax.rem(other, 4))

    near = [lax.rem(rank + d, GROUP) for d in range(1, GROUP)]
    everyone = [lax.rem(rank + d, GROUP) for d in range(GROUP)]
    after, before = lax.rem(space + 1, SPACE), lax.rem(space + SPACE - 1, SPACE)

    loads = [
        pltpu.make_async_copy(coef_hbm, coef, local_sem.at[0]),
        pltpu.make_async_copy(pat_hbm, pat, local_sem.at[1]),
        pltpu.make_async_copy(reg_hbm, reg, local_sem.at[2]),
        pltpu.make_async_copy(law_hbm, law, local_sem.at[3]),
        pltpu.make_async_copy(tab_hbm, tab, local_sem.at[4]),
        pltpu.make_async_copy(curl_hbm.at[rank], curl, local_sem.at[5]),
    ]
    for load in loads:
        load.start()
    barrier = pltpu.get_barrier_semaphore()
    for other in near:
        pl.semaphore_signal(barrier, inc=1, device_id=at(space, other), device_id_type=MESH)
    for other in everyone:
        for group in (after, before):
            pl.semaphore_signal(barrier, inc=1, device_id=at(group, other), device_id_type=MESH)

    loads[0].wait()
    loads[1].wait()
    rows = jnp.concatenate(
        [jnp.broadcast_to(pat[e : e + 1, :], (2 * LINKS, LINKS)) for e in range(TILES)], axis=0
    )
    row = lax.broadcasted_iota(jnp.int32, (TILES * LINKS * 2, LINKS), 0)
    col = lax.broadcasted_iota(jnp.int32, (TILES * LINKS * 2, LINKS), 1)
    spot = jnp.sum(jnp.where(row // 2 % LINKS == col, rows, 0), axis=1, keepdims=True)
    row = lax.broadcasted_iota(jnp.int32, (TILES * LINKS * 2, TILES * 2), 0)
    col = lax.broadcasted_iota(jnp.int32, (TILES * LINKS * 2, TILES * 2), 1)
    hits = jnp.where((spot == col // 2 + 1) & (row % 2 == col % 2), 1.0, 0.0)
    own = coef[...].astype(F32)
    own = jnp.concatenate([own[:, w * TILE : (w + 1) * TILE] for w in range(TILES)], axis=0)
    picked = jnp.dot(hits.astype(BF16), own.astype(BF16), preferred_element_type=F32)
    picks[...] = picked.reshape(TILES, 2 * LINKS, TILE).astype(BF16)
    for e in range(TILES):
        pass
    spread = hits.T.astype(BF16)
    spread = jnp.concatenate([spread, spread], axis=1)

    own_row = lax.broadcasted_iota(jnp.int32, (TILES, LINKS), 0) == rank
    links = jnp.sum(jnp.where(own_row, pat[...], 0), axis=0, keepdims=True)
    loads[2].wait()
    loads[3].wait()
    region = reg[...].reshape(1, TILES)
    lane = lax.broadcasted_iota(jnp.int32, (1, TILES), 1)
    region = jnp.sum(jnp.where(lane == rank, region, 0), axis=1, keepdims=True)
    lane = lax.broadcasted_iota(jnp.int32, (3, 4), 1)
    own_law = jnp.sum(jnp.where(lane == region, law[...], 0.0), axis=1, keepdims=True)
    base, knee, rise = own_law[0:1], own_law[1:2], own_law[2:3]
    loads[4].wait()
    lane = lax.broadcasted_iota(jnp.int32, (1, 2 * PARTS), 1)
    halo_table = []
    for k in range(LINKS):
        link = links[:, k : k + 1]
        mask = jnp.where(link == jnp.where(lane < PARTS, 0, TILES + 1), 1.0, 0.0)
        for piece in range(2):
            at_row = (piece * LINKS + k) * HALF
            halo_table.append(
                (piece, k, tab[at_row : at_row + HALF, TILE : TILE + 2 * PARTS].astype(F32) * mask)
            )
    halo_table = jnp.concatenate([v for _, _, v in sorted(halo_table, key=lambda v: v[:2])], axis=0)
    table = jnp.concatenate([tab[0:256, 0:TILE], halo_table.astype(BF16)], axis=1)
    back = tab[256:288, 0 : 3 * HALF]
    loads[5].wait()

    pl.semaphore_wait(barrier, GROUP - 1 + 2 * GROUP)

    for other in near:
        pltpu.make_async_remote_copy(
            src_ref=picks.at[other], dst_ref=got.at[rank], send_sem=send_sem.at[0],
            recv_sem=recv_sem.at[0], device_id=at(space, other), device_id_type=MESH,
        ).start()
    first, last = coef.at[:, pl.ds(0, TILE)], coef.at[:, pl.ds((TILES - 1) * TILE, TILE)]
    for other in everyone:
        pltpu.make_async_remote_copy(
            src_ref=last, dst_ref=low_got.at[rank], send_sem=send_sem.at[1],
            recv_sem=recv_sem.at[1], device_id=at(after, other), device_id_type=MESH,
        ).start()
        pltpu.make_async_remote_copy(
            src_ref=first, dst_ref=high_got.at[rank], send_sem=send_sem.at[2],
            recv_sem=recv_sem.at[2], device_id=at(before, other), device_id_type=MESH,
        ).start()
    got[rank] = picks[rank]

    def total(src, dst, i):
        return pltpu.make_async_remote_copy(
            src_ref=src, dst_ref=dst, send_sem=send_sem.at[i], recv_sem=recv_sem.at[i],
            device_id=at(space, near[0]), device_id_type=MESH,
        )

    done = [
        total(picks.at[pl.ds(0, GROUP - 1)], got.at[pl.ds(0, GROUP - 1)], 0),
        total(low_got, low_got, 1),
        total(high_got, high_got, 2),
    ]
    for d in done:
        d.wait_recv()

    halo = [ref[...].astype(F32).reshape(PARTS, TILE).astype(BF16) for ref in (low_got, high_got)]
    window = jnp.concatenate([got[...].reshape(TILES * LINKS * 2, TILE), *halo], axis=0)
    waves = jnp.dot(table, window, preferred_element_type=F32)
    waves = waves[: LINKS * HALF] + waves[LINKS * HALF :]
    waves = jnp.concatenate([waves[k * HALF : (k + 1) * HALF] for k in range(LINKS)], axis=1)
    blocks = curl[...].reshape(LINKS * TILE, COMP)
    density = jnp.dot(
        jnp.concatenate(split(waves), axis=0), blocks, preferred_element_type=F32
    )
    density = density[:HALF] + density[HALF:]
    comps = [density[:, c * TILE : (c + 1) * TILE] for c in range(3)]
    square = comps[0] * comps[0] + comps[1] * comps[1] + comps[2] * comps[2]
    reluct = base + rise * square / (square + knee)
    field = jnp.concatenate([reluct * c for c in comps], axis=1)
    high, low = split(field)
    harmonic = jnp.dot(back, jnp.concatenate([high, high, low], axis=0), preferred_element_type=F32)
    contrib = lax.dot_general(
        harmonic.astype(BF16), blocks, (((1,), (1,)), ((), ())), preferred_element_type=F32
    )
    for k in range(LINKS):
        for p in range(2):
            flow[pl.ds(2 * k + p, GROUP, stride=2 * LINKS), :] = contrib[
                p * GROUP : (p + 1) * GROUP, k * TILE : (k + 1) * TILE
            ]
    for side, spot in enumerate((0, TILES + 1)):
        edge = jnp.zeros((PARTS, TILE), F32)
        for k in range(LINKS):
            edge = edge + jnp.where(
                links[:, k : k + 1] == spot, contrib[:, k * TILE : (k + 1) * TILE], 0.0
            )
        for p in range(2):
            edge_flow[side, :, p, :] = edge[p * GROUP : (p + 1) * GROUP]

    def block(ref, which):
        return ref.at[pl.ds(pl.multiple_of(which * 8, 8), 8)]

    for other in everyone:
        pltpu.make_async_remote_copy(
            src_ref=edge_flow.at[0, other], dst_ref=high_flow.at[rank], send_sem=send_sem.at[3],
            recv_sem=recv_sem.at[3], device_id=at(before, other), device_id_type=MESH,
        ).start()
        pltpu.make_async_remote_copy(
            src_ref=edge_flow.at[1, other], dst_ref=low_flow.at[rank], send_sem=send_sem.at[4],
            recv_sem=recv_sem.at[4], device_id=at(after, other), device_id_type=MESH,
        ).start()
    for other in near:
        pltpu.make_async_remote_copy(
            src_ref=block(flow, other), dst_ref=block(flow_got, rank), send_sem=send_sem.at[5],
            recv_sem=recv_sem.at[5], device_id=at(space, other), device_id_type=MESH,
        ).start()
    mine = pl.ds(pl.multiple_of(rank * 8, 8), 8)
    flow_got[mine, :] = flow[mine, :]

    done += [
        total(edge_flow.at[0], high_flow, 3),
        total(edge_flow.at[1], low_flow, 4),
        total(flow.at[pl.ds(0, 8 * (GROUP - 1))], flow_got.at[pl.ds(0, 8 * (GROUP - 1))], 5),
    ]
    for d in done[3:]:
        d.wait_recv()
    owned = jnp.dot(
        spread, jnp.concatenate(split(flow_got[...]), axis=0), preferred_element_type=F32
    )
    low_sum, high_sum = low_flow[0], high_flow[0]
    for e in range(1, TILES):
        low_sum, high_sum = low_sum + low_flow[e], high_sum + high_flow[e]
    for w in range(TILES):
        piece = owned[2 * w : 2 * w + 2]
        if w == 0:
            piece = piece + low_sum
        if w == TILES - 1:
            piece = piece + high_sum
        out_ref[:, w * TILE : (w + 1) * TILE] = piece
    for d in done:
        d.wait_send()


def per_device(coeffs, curl_tiles, pattern, region_ids, material_law, source):
    anywhere = pl.BlockSpec(memory_space=pltpu.HBM)
    total = pl.pallas_call(
        kernel,
        out_shape=jax.ShapeDtypeStruct(source.shape, F32),
        in_specs=[anywhere] * 6,
        out_specs=pl.BlockSpec(memory_space=pltpu.VMEM),
        scratch_shapes=[
            pltpu.VMEM((2, TILES * TILE), BF16),
            pltpu.VMEM((LINKS, TILE, COMP), BF16),
            pltpu.VMEM((TILES, LINKS), jnp.int32),
            pltpu.VMEM((TILES,), jnp.int32),
            pltpu.VMEM((3, 4), F32),
            pltpu.VMEM((288, 256), BF16),
            pltpu.VMEM((TILES, 2 * LINKS, TILE), BF16),
            pltpu.VMEM((GROUP, 2 * LINKS, TILE), BF16),
            pltpu.VMEM((GROUP, 2, TILE), BF16),
            pltpu.VMEM((GROUP, 2, TILE), BF16),
            pltpu.VMEM((8, TILE), F32),
            pltpu.VMEM((GROUP * 8, TILE), F32),
            pltpu.VMEM((GROUP * 8, TILE), F32),
            pltpu.VMEM((2, GROUP, 2, TILE), F32),
            pltpu.VMEM((GROUP, 2, TILE), F32),
            pltpu.VMEM((GROUP, 2, TILE), F32),
            pltpu.SemaphoreType.DMA((6,)),
            pltpu.SemaphoreType.DMA((6,)),
            pltpu.SemaphoreType.DMA((6,)),
        ],
        compiler_params=pltpu.CompilerParams(collective_id=0, has_side_effects=True),
        name="residual",
    )(coeffs, curl_tiles, pattern, region_ids, material_law, jnp.asarray(tables()))
    return total - source


def solution(mesh):
    placed = (
        P(("harm", "samp"), "space"),
        P("space", None, None, None),
        P("space", None),
        P("space"),
        P(),
        P(("harm", "samp"), "space"),
    )
    return jax.shard_map(
        per_device,
        mesh=mesh,
        in_specs=placed,
        out_specs=P(("harm", "samp"), "space"),
        check_vma=False,
    )
```

```python
import math

import jax
import jax.numpy as jnp
import ml_dtypes
import numpy as np
from jax import lax
from jax.experimental import pallas as pl
from jax.experimental.pallas import tpu as pltpu
from jax.sharding import PartitionSpec as P

SAMPLES = 64
HALF = SAMPLES // 2
PARTS = 32
GROUP = 16
SPACE = 16
TILES = 16
LINKS = 4
TILE = 128
COMP = 3 * TILE
MESH = pl.DeviceIdType.MESH
F32, BF16 = jnp.float32, jnp.bfloat16


def two_pieces(table):
    high = table.astype(ml_dtypes.bfloat16)
    low = (table - high.astype(np.float64)).astype(ml_dtypes.bfloat16)
    return high, low


def tables():
    t = np.arange(HALF)[:, None]
    q = np.arange(PARTS)[None, :]
    phase = ((2 * (q // 2) + 1) * t % SAMPLES) * (2.0 * math.pi / SAMPLES)
    transform = np.where(q % 2 == 0, np.cos(phase), np.sin(phase))
    main = np.zeros((LINKS, HALF, GROUP, LINKS, 2))
    for k in range(LINKS):
        main[k, :, :, k, :] = transform.reshape(HALF, GROUP, 2)
    forward = np.concatenate(
        [
            main.reshape(LINKS * HALF, GROUP * LINKS * 2),
            np.tile(transform, (LINKS, 2)),
            np.zeros((LINKS * HALF, 64)),
        ],
        axis=1,
    )
    back = (4.0 / SAMPLES) * transform.reshape(HALF, GROUP, 2).transpose(2, 1, 0).reshape(PARTS, HALF)
    back_high, back_low = two_pieces(back)
    back_row = np.zeros((PARTS, 256), ml_dtypes.bfloat16)
    back_row[:, : 3 * HALF] = np.concatenate([back_high, back_low, back_high], axis=1)
    return np.concatenate([*two_pieces(forward), back_row], axis=0)


def split(value):
    high = value.astype(BF16)
    return high, (value - high.astype(F32)).astype(BF16)


def kernel(
    coef_hbm, curl_hbm, pat_hbm, reg_hbm, law_hbm, tab_hbm, out_ref,
    coef, curl, pat, reg, law, tab, picks, got, low_got, high_got, sums,
    flow, flow_got, edge_flow, low_flow, high_flow, local_sem, send_sem, recv_sem,
):
    harm, space, samp = lax.axis_index("harm"), lax.axis_index("space"), lax.axis_index("samp")
    rank = harm * 4 + samp

    def at(group, other):
        return (other // 4, group, lax.rem(other, 4))

    place = harm // 2 * 4 + samp
    core = lax.rem(harm, 2)

    def peer(step, swap):
        there = lax.rem(place + step, 8)
        return (there // 4 * 2 + lax.rem(core + swap, 2)) * 4 + lax.rem(there, 4)

    everyone = [peer(step, swap) for step in (4, 3, 5, 2, 6, 1, 7, 0) for swap in (1, 0)]
    near = everyone[:-1]
    after, before = lax.rem(space + 1, SPACE), lax.rem(space + SPACE - 1, SPACE)

    loads = [
        pltpu.make_async_copy(coef_hbm, coef, local_sem.at[0]),
        pltpu.make_async_copy(pat_hbm, pat, local_sem.at[1]),
        pltpu.make_async_copy(reg_hbm, reg, local_sem.at[2]),
        pltpu.make_async_copy(law_hbm, law, local_sem.at[3]),
        pltpu.make_async_copy(tab_hbm, tab, local_sem.at[4]),
        pltpu.make_async_copy(curl_hbm.at[rank], curl, local_sem.at[5]),
    ]
    for load in loads:
        load.start()
    barrier = pltpu.get_barrier_semaphore()
    for group in (after, before):
        for other in everyone:
            pl.semaphore_signal(barrier, inc=1, device_id=at(group, other), device_id_type=MESH)
    for other in near:
        pl.semaphore_signal(barrier, inc=1, device_id=at(space, other), device_id_type=MESH)

    loads[0].wait()
    loads[1].wait()
    pattern = pat[...].T
    rows = jnp.concatenate(
        [jnp.broadcast_to(pattern[e : e + 1, :], (2 * LINKS, LINKS)) for e in range(TILES)], axis=0
    )
    row = lax.broadcasted_iota(jnp.int32, (TILES * LINKS * 2, LINKS), 0)
    col = lax.broadcasted_iota(jnp.int32, (TILES * LINKS * 2, LINKS), 1)
    spot = jnp.sum(jnp.where(row // 2 % LINKS == col, rows, 0), axis=1, keepdims=True)
    row = lax.broadcasted_iota(jnp.int32, (TILES * LINKS * 2, TILES * 2), 0)
    col = lax.broadcasted_iota(jnp.int32, (TILES * LINKS * 2, TILES * 2), 1)
    hits = jnp.where((spot == col // 2 + 1) & (row % 2 == col % 2), 1.0, 0.0)
    own = coef[...].astype(F32)
    own = jnp.concatenate([own[:, w * TILE : (w + 1) * TILE] for w in range(TILES)], axis=0)
    picked = jnp.dot(hits.astype(BF16), own.astype(BF16), preferred_element_type=F32)
    picks[...] = picked.reshape(TILES, 2 * LINKS, TILE).astype(BF16)
    spread = hits.T.astype(BF16)
    spread = jnp.concatenate([spread, spread], axis=1)

    own_row = lax.broadcasted_iota(jnp.int32, (TILES, LINKS), 0) == rank
    links = jnp.sum(jnp.where(own_row, pattern, 0), axis=0, keepdims=True)
    loads[2].wait()
    loads[3].wait()
    region = reg[...].reshape(1, TILES)
    lane = lax.broadcasted_iota(jnp.int32, (1, TILES), 1)
    region = jnp.sum(jnp.where(lane == rank, region, 0), axis=1, keepdims=True)
    lane = lax.broadcasted_iota(jnp.int32, (3, 4), 1)
    own_law = jnp.sum(jnp.where(lane == region, law[...], 0.0), axis=1, keepdims=True)
    base, knee, rise = own_law[0:1], own_law[1:2], own_law[2:3]
    loads[4].wait()
    lane = lax.broadcasted_iota(jnp.int32, (1, 2 * PARTS), 1)
    halo_table = []
    for k in range(LINKS):
        link = links[:, k : k + 1]
        mask = jnp.where(link == jnp.where(lane < PARTS, 0, TILES + 1), 1.0, 0.0)
        for piece in range(2):
            at_row = (piece * LINKS + k) * HALF
            halo_table.append(
                (piece, k, tab[at_row : at_row + HALF, TILE : TILE + 2 * PARTS].astype(F32) * mask)
            )
    halo_table = jnp.concatenate([v for _, _, v in sorted(halo_table, key=lambda v: v[:2])], axis=0)
    table = jnp.concatenate([tab[0:256, 0:TILE], halo_table.astype(BF16)], axis=1)
    back = tab[256:288, 0 : 3 * HALF]
    loads[5].wait()

    pl.semaphore_wait(barrier, GROUP - 1 + 2 * GROUP)

    first, last = coef.at[:, pl.ds(0, TILE)], coef.at[:, pl.ds((TILES - 1) * TILE, TILE)]
    for other in everyone:
        pltpu.make_async_remote_copy(
            src_ref=first, dst_ref=high_got.at[rank], send_sem=send_sem.at[2],
            recv_sem=recv_sem.at[2], device_id=at(before, other), device_id_type=MESH,
        ).start()
    for other in everyone:
        pltpu.make_async_remote_copy(
            src_ref=last, dst_ref=low_got.at[rank], send_sem=send_sem.at[1],
            recv_sem=recv_sem.at[1], device_id=at(after, other), device_id_type=MESH,
        ).start()
    for other in near:
        pltpu.make_async_remote_copy(
            src_ref=picks.at[other], dst_ref=got.at[rank], send_sem=send_sem.at[0],
            recv_sem=recv_sem.at[0], device_id=at(space, other), device_id_type=MESH,
        ).start()
    got[rank] = picks[rank]

    def total(src, dst, i):
        return pltpu.make_async_remote_copy(
            src_ref=src, dst_ref=dst, send_sem=send_sem.at[i], recv_sem=recv_sem.at[i],
            device_id=at(space, near[0]), device_id_type=MESH,
        )

    done = [
        total(picks.at[pl.ds(0, GROUP - 1)], got.at[pl.ds(0, GROUP - 1)], 0),
        total(low_got, low_got, 1),
        total(high_got, high_got, 2),
    ]
    for d in done:
        d.wait_recv()

    halo = [ref[...].astype(F32).reshape(PARTS, TILE).astype(BF16) for ref in (low_got, high_got)]
    window = jnp.concatenate([got[...].reshape(TILES * LINKS * 2, TILE), *halo], axis=0)
    waves = jnp.dot(table, window, preferred_element_type=F32)
    waves = waves[: LINKS * HALF] + waves[LINKS * HALF :]
    waves = jnp.concatenate([waves[k * HALF : (k + 1) * HALF] for k in range(LINKS)], axis=1)
    blocks = curl[...].reshape(LINKS * TILE, COMP)
    density = jnp.dot(
        jnp.concatenate(split(waves), axis=0), blocks, preferred_element_type=F32
    )
    density = density[:HALF] + density[HALF:]
    comps = [density[:, c * TILE : (c + 1) * TILE] for c in range(3)]
    square = comps[0] * comps[0] + comps[1] * comps[1] + comps[2] * comps[2]
    reluct = base + rise * square / (square + knee)
    field = jnp.concatenate([reluct * c for c in comps], axis=1)
    high, low = split(field)
    harmonic = jnp.dot(back, jnp.concatenate([high, high, low], axis=0), preferred_element_type=F32)
    contrib = lax.dot_general(
        harmonic.astype(BF16), blocks, (((1,), (1,)), ((), ())), preferred_element_type=F32
    )
    for k in range(LINKS):
        for p in range(2):
            flow[pl.ds(2 * k + p, GROUP, stride=2 * LINKS), :] = contrib[
                p * GROUP : (p + 1) * GROUP, k * TILE : (k + 1) * TILE
            ]
    for side, spot in enumerate((0, TILES + 1)):
        edge = jnp.zeros((PARTS, TILE), F32)
        for k in range(LINKS):
            edge = edge + jnp.where(
                links[:, k : k + 1] == spot, contrib[:, k * TILE : (k + 1) * TILE], 0.0
            )
        for p in range(2):
            edge_flow[side, :, p, :] = edge[p * GROUP : (p + 1) * GROUP]

    def block(ref, which):
        return ref.at[pl.ds(pl.multiple_of(which * 8, 8), 8)]

    for other in everyone:
        pltpu.make_async_remote_copy(
            src_ref=edge_flow.at[1, other], dst_ref=low_flow.at[rank], send_sem=send_sem.at[4],
            recv_sem=recv_sem.at[4], device_id=at(after, other), device_id_type=MESH,
        ).start()
    for other in everyone:
        pltpu.make_async_remote_copy(
            src_ref=edge_flow.at[0, other], dst_ref=high_flow.at[rank], send_sem=send_sem.at[3],
            recv_sem=recv_sem.at[3], device_id=at(before, other), device_id_type=MESH,
        ).start()
    for other in near:
        pltpu.make_async_remote_copy(
            src_ref=block(flow, other), dst_ref=block(flow_got, rank), send_sem=send_sem.at[5],
            recv_sem=recv_sem.at[5], device_id=at(space, other), device_id_type=MESH,
        ).start()
    mine = pl.ds(pl.multiple_of(rank * 8, 8), 8)
    flow_got[mine, :] = flow[mine, :]

    done += [
        total(edge_flow.at[0], high_flow, 3),
        total(edge_flow.at[1], low_flow, 4),
        total(flow.at[pl.ds(0, 8 * (GROUP - 1))], flow_got.at[pl.ds(0, 8 * (GROUP - 1))], 5),
    ]
    for d in done[3:]:
        d.wait_recv()
    owned = jnp.dot(
        spread, jnp.concatenate(split(flow_got[...]), axis=0), preferred_element_type=F32
    )
    low_sum, high_sum = low_flow[0], high_flow[0]
    for e in range(1, TILES):
        low_sum, high_sum = low_sum + low_flow[e], high_sum + high_flow[e]
    for w in range(TILES):
        piece = owned[2 * w : 2 * w + 2]
        if w == 0:
            piece = piece + low_sum
        if w == TILES - 1:
            piece = piece + high_sum
        out_ref[:, w * TILE : (w + 1) * TILE] = piece
    for d in done:
        d.wait_send()


def per_device(coeffs, curl_tiles, pattern, region_ids, material_law, source):
    anywhere = pl.BlockSpec(memory_space=pltpu.HBM)
    total = pl.pallas_call(
        kernel,
        out_shape=pltpu.VMEM(source.shape, F32),
        in_specs=[anywhere] * 6,
        out_specs=pl.BlockSpec(memory_space=pltpu.VMEM),
        scratch_shapes=[
            pltpu.VMEM((2, TILES * TILE), BF16),
            pltpu.VMEM((LINKS, TILE, COMP), BF16),
            pltpu.VMEM((LINKS, TILES), jnp.int32),
            pltpu.VMEM((TILES,), jnp.int32),
            pltpu.VMEM((3, 4), F32),
            pltpu.VMEM((288, 256), BF16),
            pltpu.VMEM((TILES, 2 * LINKS, TILE), BF16),
            pltpu.VMEM((GROUP, 2 * LINKS, TILE), BF16),
            pltpu.VMEM((GROUP, 2, TILE), BF16),
            pltpu.VMEM((GROUP, 2, TILE), BF16),
            pltpu.VMEM((8, TILE), F32),
            pltpu.VMEM((GROUP * 8, TILE), F32),
            pltpu.VMEM((GROUP * 8, TILE), F32),
            pltpu.VMEM((2, GROUP, 2, TILE), F32),
            pltpu.VMEM((GROUP, 2, TILE), F32),
            pltpu.VMEM((GROUP, 2, TILE), F32),
            pltpu.SemaphoreType.DMA((6,)),
            pltpu.SemaphoreType.DMA((6,)),
            pltpu.SemaphoreType.DMA((6,)),
        ],
        compiler_params=pltpu.CompilerParams(collective_id=0, has_side_effects=True),
        name="residual",
    )(coeffs, curl_tiles, pattern.T, region_ids, material_law, jnp.asarray(tables()))
    return total - source


def solution(mesh):
    placed = (
        P(("harm", "samp"), "space"),
        P("space", None, None, None),
        P("space", None),
        P("space"),
        P(),
        P(("harm", "samp"), "space"),
    )
    return jax.shard_map(
        per_device,
        mesh=mesh,
        in_specs=placed,
        out_specs=P(("harm", "samp"), "space"),
        check_vma=False,
    )
```

```python
import math

import jax
import jax.numpy as jnp
import ml_dtypes
import numpy as np
from jax import lax
from jax.experimental import pallas as pl
from jax.experimental.pallas import tpu as pltpu
from jax.sharding import PartitionSpec as P

SAMPLES = 64
HALF = SAMPLES // 2
PARTS = 32
GROUP = 16
SPACE = 16
TILES = 16
LINKS = 4
TILE = 128
COMP = 3 * TILE
MESH = pl.DeviceIdType.MESH
F32, BF16 = jnp.float32, jnp.bfloat16


def two_pieces(table):
    high = table.astype(ml_dtypes.bfloat16)
    low = (table - high.astype(np.float64)).astype(ml_dtypes.bfloat16)
    return high, low


def tables():
    t = np.arange(HALF)[:, None]
    q = np.arange(PARTS)[None, :]
    phase = ((2 * (q // 2) + 1) * t % SAMPLES) * (2.0 * math.pi / SAMPLES)
    transform = np.where(q % 2 == 0, np.cos(phase), np.sin(phase))
    main = np.zeros((LINKS, HALF, GROUP, LINKS, 2))
    for k in range(LINKS):
        main[k, :, :, k, :] = transform.reshape(HALF, GROUP, 2)
    forward = np.concatenate(
        [
            main.reshape(LINKS * HALF, GROUP * LINKS * 2),
            np.tile(transform, (LINKS, 2)),
            np.zeros((LINKS * HALF, 64)),
        ],
        axis=1,
    )
    back = (4.0 / SAMPLES) * transform.reshape(HALF, GROUP, 2).transpose(2, 1, 0).reshape(PARTS, HALF)
    back_high, back_low = two_pieces(back)
    back_row = np.zeros((PARTS, 256), ml_dtypes.bfloat16)
    back_row[:, : 3 * HALF] = np.concatenate([back_high, back_low, back_high], axis=1)
    return np.concatenate([*two_pieces(forward), back_row], axis=0)


def split(value):
    high = value.astype(BF16)
    return high, (value - high.astype(F32)).astype(BF16)


def kernel(
    coef_hbm, curl_hbm, pat_hbm, reg_hbm, law_hbm, tab_hbm, out_ref,
    coef, curl, pat, reg, law, tab, picks, got, low_got, high_got, sums,
    flow, flow_got, edge_flow, low_flow, high_flow, local_sem, send_sem, recv_sem, ready, firsts,
):
    harm, space, samp = lax.axis_index("harm"), lax.axis_index("space"), lax.axis_index("samp")
    rank = harm * 4 + samp

    def at(group, other):
        return (other // 4, group, lax.rem(other, 4))

    place = harm // 2 * 4 + samp
    core = lax.rem(harm, 2)

    def peer(step, swap):
        there = lax.rem(place + step, 8)
        return (there // 4 * 2 + lax.rem(core + swap, 2)) * 4 + lax.rem(there, 4)

    everyone = [peer(step, swap) for step in (4, 3, 5, 2, 6, 1, 7, 0) for swap in (1, 0)]
    near = everyone[:-1]
    after, before = lax.rem(space + 1, SPACE), lax.rem(space + SPACE - 1, SPACE)

    loads = [
        pltpu.make_async_copy(coef_hbm, coef, local_sem.at[0]),
        pltpu.make_async_copy(pat_hbm, pat, local_sem.at[1]),
        pltpu.make_async_copy(reg_hbm, reg, local_sem.at[2]),
        pltpu.make_async_copy(law_hbm, law, local_sem.at[3]),
        pltpu.make_async_copy(tab_hbm, tab, local_sem.at[4]),
        pltpu.make_async_copy(curl_hbm.at[rank], curl, local_sem.at[5]),
    ]
    for load in loads:
        load.start()
    barrier = pltpu.get_barrier_semaphore()
    for other in everyone:
        pl.semaphore_signal(barrier, inc=1, device_id=at(before, other), device_id_type=MESH)
    for other in near:
        pl.semaphore_signal(barrier, inc=1, device_id=at(space, other), device_id_type=MESH)

    loads[0].wait()
    loads[1].wait()
    pattern = pat[...].T
    rows = jnp.concatenate(
        [jnp.broadcast_to(pattern[e : e + 1, :], (2 * LINKS, LINKS)) for e in range(TILES)], axis=0
    )
    row = lax.broadcasted_iota(jnp.int32, (TILES * LINKS * 2, LINKS), 0)
    col = lax.broadcasted_iota(jnp.int32, (TILES * LINKS * 2, LINKS), 1)
    spot = jnp.sum(jnp.where(row // 2 % LINKS == col, rows, 0), axis=1, keepdims=True)
    row = lax.broadcasted_iota(jnp.int32, (TILES * LINKS * 2, TILES * 2), 0)
    col = lax.broadcasted_iota(jnp.int32, (TILES * LINKS * 2, TILES * 2), 1)
    hits = jnp.where((spot == col // 2 + 1) & (row % 2 == col % 2), 1.0, 0.0)
    own = coef[...].astype(F32)
    own = jnp.concatenate([own[:, w * TILE : (w + 1) * TILE] for w in range(TILES)], axis=0)
    picked = jnp.dot(hits.astype(BF16), own.astype(BF16), preferred_element_type=F32)
    picks[...] = picked.reshape(TILES, 2 * LINKS, TILE).astype(BF16)
    spread = hits.T.astype(BF16)
    spread = jnp.concatenate([spread, spread], axis=1)

    own_row = lax.broadcasted_iota(jnp.int32, (TILES, LINKS), 0) == rank
    links = jnp.sum(jnp.where(own_row, pattern, 0), axis=0, keepdims=True)
    loads[2].wait()
    loads[3].wait()
    region = reg[...].reshape(1, TILES)
    lane = lax.broadcasted_iota(jnp.int32, (1, TILES), 1)
    region = jnp.sum(jnp.where(lane == rank, region, 0), axis=1, keepdims=True)
    lane = lax.broadcasted_iota(jnp.int32, (3, 4), 1)
    own_law = jnp.sum(jnp.where(lane == region, law[...], 0.0), axis=1, keepdims=True)
    base, knee, rise = own_law[0:1], own_law[1:2], own_law[2:3]
    loads[4].wait()
    lane = lax.broadcasted_iota(jnp.int32, (1, 2 * PARTS), 1)
    halo_table = []
    for k in range(LINKS):
        link = links[:, k : k + 1]
        mask = jnp.where(link == jnp.where(lane < PARTS, 0, TILES + 1), 1.0, 0.0)
        for piece in range(2):
            at_row = (piece * LINKS + k) * HALF
            halo_table.append(
                (piece, k, tab[at_row : at_row + HALF, TILE : TILE + 2 * PARTS].astype(F32) * mask)
            )
    halo_table = jnp.concatenate([v for _, _, v in sorted(halo_table, key=lambda v: v[:2])], axis=0)
    table = jnp.concatenate([tab[0:256, 0:TILE], halo_table.astype(BF16)], axis=1)
    back = tab[256:288, 0 : 3 * HALF]
    loads[5].wait()

    pl.semaphore_wait(barrier, GROUP - 1 + GROUP)

    pl.semaphore_signal(ready, inc=1, device_id=at(after, rank), device_id_type=MESH)
    first, last = coef.at[:, pl.ds(0, TILE)], coef.at[:, pl.ds((TILES - 1) * TILE, TILE)]
    for other in near:
        pltpu.make_async_remote_copy(
            src_ref=first, dst_ref=firsts.at[rank], send_sem=send_sem.at[6],
            recv_sem=recv_sem.at[6], device_id=at(space, other), device_id_type=MESH,
        ).start()
    for other in everyone:
        pltpu.make_async_remote_copy(
            src_ref=last, dst_ref=low_got.at[rank], send_sem=send_sem.at[1],
            recv_sem=recv_sem.at[1], device_id=at(after, other), device_id_type=MESH,
        ).start()
    for other in near:
        pltpu.make_async_remote_copy(
            src_ref=picks.at[other], dst_ref=got.at[rank], send_sem=send_sem.at[0],
            recv_sem=recv_sem.at[0], device_id=at(space, other), device_id_type=MESH,
        ).start()
    firsts[rank] = coef[:, 0:TILE]
    got[rank] = picks[rank]

    def total(src, dst, i):
        return pltpu.make_async_remote_copy(
            src_ref=src, dst_ref=dst, send_sem=send_sem.at[i], recv_sem=recv_sem.at[i],
            device_id=at(space, near[0]), device_id_type=MESH,
        )

    done = [
        total(picks.at[pl.ds(0, GROUP - 1)], got.at[pl.ds(0, GROUP - 1)], 0),
        total(low_got, low_got, 1),
        pltpu.make_async_remote_copy(
            src_ref=firsts, dst_ref=high_got, send_sem=send_sem.at[2], recv_sem=recv_sem.at[2],
            device_id=at(before, rank), device_id_type=MESH,
        ),
        total(firsts.at[pl.ds(0, GROUP - 1)], firsts.at[pl.ds(0, GROUP - 1)], 6),
    ]
    done[3].wait_recv()
    pl.semaphore_wait(ready, 1)
    done[2].start()
    for d in done[:3]:
        d.wait_recv()

    halo = [ref[...].astype(F32).reshape(PARTS, TILE).astype(BF16) for ref in (low_got, high_got)]
    window = jnp.concatenate([got[...].reshape(TILES * LINKS * 2, TILE), *halo], axis=0)
    waves = jnp.dot(table, window, preferred_element_type=F32)
    waves = waves[: LINKS * HALF] + waves[LINKS * HALF :]
    waves = jnp.concatenate([waves[k * HALF : (k + 1) * HALF] for k in range(LINKS)], axis=1)
    blocks = curl[...].reshape(LINKS * TILE, COMP)
    density = jnp.dot(
        jnp.concatenate(split(waves), axis=0), blocks, preferred_element_type=F32
    )
    density = density[:HALF] + density[HALF:]
    comps = [density[:, c * TILE : (c + 1) * TILE] for c in range(3)]
    square = comps[0] * comps[0] + comps[1] * comps[1] + comps[2] * comps[2]
    reluct = base + rise * square / (square + knee)
    field = jnp.concatenate([reluct * c for c in comps], axis=1)
    high, low = split(field)
    harmonic = jnp.dot(back, jnp.concatenate([high, high, low], axis=0), preferred_element_type=F32)
    contrib = lax.dot_general(
        harmonic.astype(BF16), blocks, (((1,), (1,)), ((), ())), preferred_element_type=F32
    )
    for k in range(LINKS):
        for p in range(2):
            flow[pl.ds(2 * k + p, GROUP, stride=2 * LINKS), :] = contrib[
                p * GROUP : (p + 1) * GROUP, k * TILE : (k + 1) * TILE
            ]
    for side, spot in enumerate((0, TILES + 1)):
        edge = jnp.zeros((PARTS, TILE), F32)
        for k in range(LINKS):
            edge = edge + jnp.where(
                links[:, k : k + 1] == spot, contrib[:, k * TILE : (k + 1) * TILE], 0.0
            )
        for p in range(2):
            edge_flow[side, :, p, :] = edge[p * GROUP : (p + 1) * GROUP]

    def block(ref, which):
        return ref.at[pl.ds(pl.multiple_of(which * 8, 8), 8)]

    for other in everyone:
        pltpu.make_async_remote_copy(
            src_ref=edge_flow.at[1, other], dst_ref=low_flow.at[rank], send_sem=send_sem.at[4],
            recv_sem=recv_sem.at[4], device_id=at(after, other), device_id_type=MESH,
        ).start()
    for other in everyone:
        pltpu.make_async_remote_copy(
            src_ref=edge_flow.at[0, other], dst_ref=high_flow.at[rank], send_sem=send_sem.at[3],
            recv_sem=recv_sem.at[3], device_id=at(before, other), device_id_type=MESH,
        ).start()
    for other in near:
        pltpu.make_async_remote_copy(
            src_ref=block(flow, other), dst_ref=block(flow_got, rank), send_sem=send_sem.at[5],
            recv_sem=recv_sem.at[5], device_id=at(space, other), device_id_type=MESH,
        ).start()
    mine = pl.ds(pl.multiple_of(rank * 8, 8), 8)
    flow_got[mine, :] = flow[mine, :]

    done += [
        total(edge_flow.at[0], high_flow, 3),
        total(edge_flow.at[1], low_flow, 4),
        total(flow.at[pl.ds(0, 8 * (GROUP - 1))], flow_got.at[pl.ds(0, 8 * (GROUP - 1))], 5),
    ]
    for d in done[4:]:
        d.wait_recv()
    owned = jnp.dot(
        spread, jnp.concatenate(split(flow_got[...]), axis=0), preferred_element_type=F32
    )
    low_sum, high_sum = low_flow[0], high_flow[0]
    for e in range(1, TILES):
        low_sum, high_sum = low_sum + low_flow[e], high_sum + high_flow[e]
    for w in range(TILES):
        piece = owned[2 * w : 2 * w + 2]
        if w == 0:
            piece = piece + low_sum
        if w == TILES - 1:
            piece = piece + high_sum
        out_ref[:, w * TILE : (w + 1) * TILE] = piece
    for d in done:
        d.wait_send()


def per_device(coeffs, curl_tiles, pattern, region_ids, material_law, source):
    anywhere = pl.BlockSpec(memory_space=pltpu.HBM)
    total = pl.pallas_call(
        kernel,
        out_shape=pltpu.VMEM(source.shape, F32),
        in_specs=[anywhere] * 6,
        out_specs=pl.BlockSpec(memory_space=pltpu.VMEM),
        scratch_shapes=[
            pltpu.VMEM((2, TILES * TILE), BF16),
            pltpu.VMEM((LINKS, TILE, COMP), BF16),
            pltpu.VMEM((LINKS, TILES), jnp.int32),
            pltpu.VMEM((TILES,), jnp.int32),
            pltpu.VMEM((3, 4), F32),
            pltpu.VMEM((288, 256), BF16),
            pltpu.VMEM((TILES, 2 * LINKS, TILE), BF16),
            pltpu.VMEM((GROUP, 2 * LINKS, TILE), BF16),
            pltpu.VMEM((GROUP, 2, TILE), BF16),
            pltpu.VMEM((GROUP, 2, TILE), BF16),
            pltpu.VMEM((8, TILE), F32),
            pltpu.VMEM((GROUP * 8, TILE), F32),
            pltpu.VMEM((GROUP * 8, TILE), F32),
            pltpu.VMEM((2, GROUP, 2, TILE), F32),
            pltpu.VMEM((GROUP, 2, TILE), F32),
            pltpu.VMEM((GROUP, 2, TILE), F32),
            pltpu.SemaphoreType.DMA((6,)),
            pltpu.SemaphoreType.DMA((7,)),
            pltpu.SemaphoreType.DMA((7,)),
            pltpu.SemaphoreType.REGULAR,
            pltpu.VMEM((GROUP, 2, TILE), BF16),
        ],
        compiler_params=pltpu.CompilerParams(collective_id=0, has_side_effects=True),
        name="residual",
    )(coeffs, curl_tiles, pattern.T, region_ids, material_law, jnp.asarray(tables()))
    return total - source


def solution(mesh):
    placed = (
        P(("harm", "samp"), "space"),
        P("space", None, None, None),
        P("space", None),
        P("space"),
        P(),
        P(("harm", "samp"), "space"),
    )
    return jax.shard_map(
        per_device,
        mesh=mesh,
        in_specs=placed,
        out_specs=P(("harm", "samp"), "space"),
        check_vma=False,
    )
```

```python
import math

import jax
import jax.numpy as jnp
import ml_dtypes
import numpy as np
from jax import lax
from jax.experimental import pallas as pl
from jax.experimental.pallas import tpu as pltpu
from jax.sharding import PartitionSpec as P

SAMPLES = 64
HALF = SAMPLES // 2
PARTS = 32
GROUP = 16
SPACE = 16
TILES = 16
LINKS = 4
TILE = 128
COMP = 3 * TILE
MESH = pl.DeviceIdType.MESH
F32, BF16 = jnp.float32, jnp.bfloat16


def two_pieces(table):
    high = table.astype(ml_dtypes.bfloat16)
    low = (table - high.astype(np.float64)).astype(ml_dtypes.bfloat16)
    return high, low


def tables():
    t = np.arange(HALF)[:, None]
    q = np.arange(PARTS)[None, :]
    phase = ((2 * (q // 2) + 1) * t % SAMPLES) * (2.0 * math.pi / SAMPLES)
    transform = np.where(q % 2 == 0, np.cos(phase), np.sin(phase))
    main = np.zeros((LINKS, HALF, GROUP, LINKS, 2))
    for k in range(LINKS):
        main[k, :, :, k, :] = transform.reshape(HALF, GROUP, 2)
    forward = np.concatenate(
        [
            main.reshape(LINKS * HALF, GROUP * LINKS * 2),
            np.tile(transform, (LINKS, 2)),
            np.zeros((LINKS * HALF, 64)),
        ],
        axis=1,
    )
    back = (4.0 / SAMPLES) * transform.reshape(HALF, GROUP, 2).transpose(2, 1, 0).reshape(PARTS, HALF)
    back_high, back_low = two_pieces(back)
    back_row = np.zeros((PARTS, 256), ml_dtypes.bfloat16)
    back_row[:, : 3 * HALF] = np.concatenate([back_high, back_low, back_high], axis=1)
    return np.concatenate([*two_pieces(forward), back_row], axis=0)


def split(value):
    high = value.astype(BF16)
    return high, (value - high.astype(F32)).astype(BF16)


def kernel(
    coef_hbm, curl_hbm, pat_hbm, reg_hbm, law_hbm, tab_hbm, out_ref,
    coef, curl, pat, reg, law, tab, picks, got, low_got, high_got, sums,
    flow, flow_got, edge_flow, low_flow, high_flow, local_sem, send_sem, recv_sem, ready, firsts,
):
    harm, space, samp = lax.axis_index("harm"), lax.axis_index("space"), lax.axis_index("samp")
    rank = harm * 4 + samp

    def at(group, other):
        return (other // 4, group, lax.rem(other, 4))

    place = harm // 2 * 4 + samp
    core = lax.rem(harm, 2)

    def peer(step, swap):
        there = lax.rem(place + step, 8)
        return (there // 4 * 2 + lax.rem(core + swap, 2)) * 4 + lax.rem(there, 4)

    everyone = [peer(step, swap) for step in (4, 3, 5, 2, 6, 1, 7, 0) for swap in (1, 0)]
    near = everyone[:-1]
    after, before = lax.rem(space + 1, SPACE), lax.rem(space + SPACE - 1, SPACE)

    loads = [
        pltpu.make_async_copy(coef_hbm, coef, local_sem.at[0]),
        pltpu.make_async_copy(pat_hbm, pat, local_sem.at[1]),
        pltpu.make_async_copy(reg_hbm, reg, local_sem.at[2]),
        pltpu.make_async_copy(law_hbm, law, local_sem.at[3]),
        pltpu.make_async_copy(tab_hbm, tab, local_sem.at[4]),
        pltpu.make_async_copy(curl_hbm.at[rank], curl, local_sem.at[5]),
    ]
    for load in loads:
        load.start()
    barrier = pltpu.get_barrier_semaphore()
    for other in everyone:
        pl.semaphore_signal(barrier, inc=1, device_id=at(before, other), device_id_type=MESH)
    for other in near:
        pl.semaphore_signal(barrier, inc=1, device_id=at(space, other), device_id_type=MESH)

    loads[0].wait()
    loads[1].wait()
    pattern = pat[...].T
    rows = jnp.concatenate(
        [jnp.broadcast_to(pattern[e : e + 1, :], (2 * LINKS, LINKS)) for e in range(TILES)], axis=0
    )
    row = lax.broadcasted_iota(jnp.int32, (TILES * LINKS * 2, LINKS), 0)
    col = lax.broadcasted_iota(jnp.int32, (TILES * LINKS * 2, LINKS), 1)
    spot = jnp.sum(jnp.where(row // 2 % LINKS == col, rows, 0), axis=1, keepdims=True)
    row = lax.broadcasted_iota(jnp.int32, (TILES * LINKS * 2, TILES * 2), 0)
    col = lax.broadcasted_iota(jnp.int32, (TILES * LINKS * 2, TILES * 2), 1)
    hits = jnp.where((spot == col // 2 + 1) & (row % 2 == col % 2), 1.0, 0.0)
    own = coef[...].astype(F32)
    own = jnp.concatenate([own[:, w * TILE : (w + 1) * TILE] for w in range(TILES)], axis=0)
    picked = jnp.dot(hits.astype(BF16), own.astype(BF16), preferred_element_type=F32)
    picks[...] = picked.reshape(TILES, 2 * LINKS, TILE).astype(BF16)
    spread = hits.T.astype(BF16)
    spread = jnp.concatenate([spread, spread], axis=1)

    own_row = lax.broadcasted_iota(jnp.int32, (TILES, LINKS), 0) == rank
    links = jnp.sum(jnp.where(own_row, pattern, 0), axis=0, keepdims=True)
    loads[2].wait()
    loads[3].wait()
    region = reg[...].reshape(1, TILES)
    lane = lax.broadcasted_iota(jnp.int32, (1, TILES), 1)
    region = jnp.sum(jnp.where(lane == rank, region, 0), axis=1, keepdims=True)
    lane = lax.broadcasted_iota(jnp.int32, (3, 4), 1)
    own_law = jnp.sum(jnp.where(lane == region, law[...], 0.0), axis=1, keepdims=True)
    base, knee, rise = own_law[0:1], own_law[1:2], own_law[2:3]
    loads[4].wait()
    lane = lax.broadcasted_iota(jnp.int32, (1, 2 * PARTS), 1)
    halo_table = []
    for k in range(LINKS):
        link = links[:, k : k + 1]
        mask = jnp.where(link == jnp.where(lane < PARTS, 0, TILES + 1), 1.0, 0.0)
        for piece in range(2):
            at_row = (piece * LINKS + k) * HALF
            halo_table.append(
                (piece, k, tab[at_row : at_row + HALF, TILE : TILE + 2 * PARTS].astype(F32) * mask)
            )
    halo_table = jnp.concatenate([v for _, _, v in sorted(halo_table, key=lambda v: v[:2])], axis=0)
    table = jnp.concatenate([tab[0:256, 0:TILE], halo_table.astype(BF16)], axis=1)
    back = tab[256:288, 0 : 3 * HALF]
    loads[5].wait()

    pl.semaphore_wait(barrier, GROUP - 1 + GROUP)

    hub = rank - 4 * core + 4
    pl.semaphore_signal(ready, inc=1, device_id=at(after, hub), device_id_type=MESH)
    first, last = coef.at[:, pl.ds(0, TILE)], coef.at[:, pl.ds((TILES - 1) * TILE, TILE)]

    def to_hub(other):
        return pltpu.make_async_remote_copy(
            src_ref=first, dst_ref=firsts.at[rank], send_sem=send_sem.at[6],
            recv_sem=recv_sem.at[6], device_id=at(space, other), device_id_type=MESH,
        )

    hubs = [peer(step, 1 - core) for step in (4, 3, 5, 2, 6, 1, 7)]
    for other in hubs:
        to_hub(other).start()

    @pl.when(core == 0)
    def _():
        to_hub(hub).start()

    for other in everyone:
        pltpu.make_async_remote_copy(
            src_ref=last, dst_ref=low_got.at[rank], send_sem=send_sem.at[1],
            recv_sem=recv_sem.at[1], device_id=at(after, other), device_id_type=MESH,
        ).start()
    for other in near:
        pltpu.make_async_remote_copy(
            src_ref=picks.at[other], dst_ref=got.at[rank], send_sem=send_sem.at[0],
            recv_sem=recv_sem.at[0], device_id=at(space, other), device_id_type=MESH,
        ).start()
    firsts[rank] = coef[:, 0:TILE]
    got[rank] = picks[rank]

    def total(src, dst, i):
        return pltpu.make_async_remote_copy(
            src_ref=src, dst_ref=dst, send_sem=send_sem.at[i], recv_sem=recv_sem.at[i],
            device_id=at(space, near[0]), device_id_type=MESH,
        )

    done = [
        total(picks.at[pl.ds(0, GROUP - 1)], got.at[pl.ds(0, GROUP - 1)], 0),
        total(low_got, low_got, 1),
        total(high_got, high_got, 2),
    ]

    def from_hub(other):
        return pltpu.make_async_remote_copy(
            src_ref=firsts, dst_ref=high_got, send_sem=send_sem.at[2], recv_sem=recv_sem.at[2],
            device_id=at(before, other), device_id_type=MESH,
        )

    gathered = total(firsts.at[pl.ds(0, GROUP - 1)], firsts.at[pl.ds(0, GROUP - 1)], 6)

    @pl.when(core == 1)
    def _():
        gathered.wait_recv()
        pl.semaphore_wait(ready, 2)
        from_hub(rank - 4).start()
        from_hub(rank).start()

    for d in done[:3]:
        d.wait_recv()

    halo = [ref[...].astype(F32).reshape(PARTS, TILE).astype(BF16) for ref in (low_got, high_got)]
    window = jnp.concatenate([got[...].reshape(TILES * LINKS * 2, TILE), *halo], axis=0)
    waves = jnp.dot(table, window, preferred_element_type=F32)
    waves = waves[: LINKS * HALF] + waves[LINKS * HALF :]
    waves = jnp.concatenate([waves[k * HALF : (k + 1) * HALF] for k in range(LINKS)], axis=1)
    blocks = curl[...].reshape(LINKS * TILE, COMP)
    density = jnp.dot(
        jnp.concatenate(split(waves), axis=0), blocks, preferred_element_type=F32
    )
    density = density[:HALF] + density[HALF:]
    comps = [density[:, c * TILE : (c + 1) * TILE] for c in range(3)]
    square = comps[0] * comps[0] + comps[1] * comps[1] + comps[2] * comps[2]
    reluct = base + rise * square / (square + knee)
    field = jnp.concatenate([reluct * c for c in comps], axis=1)
    high, low = split(field)
    harmonic = jnp.dot(back, jnp.concatenate([high, high, low], axis=0), preferred_element_type=F32)
    contrib = lax.dot_general(
        harmonic.astype(BF16), blocks, (((1,), (1,)), ((), ())), preferred_element_type=F32
    )
    for k in range(LINKS):
        for p in range(2):
            flow[pl.ds(2 * k + p, GROUP, stride=2 * LINKS), :] = contrib[
                p * GROUP : (p + 1) * GROUP, k * TILE : (k + 1) * TILE
            ]
    for side, spot in enumerate((0, TILES + 1)):
        edge = jnp.zeros((PARTS, TILE), F32)
        for k in range(LINKS):
            edge = edge + jnp.where(
                links[:, k : k + 1] == spot, contrib[:, k * TILE : (k + 1) * TILE], 0.0
            )
        for p in range(2):
            edge_flow[side, :, p, :] = edge[p * GROUP : (p + 1) * GROUP]

    def block(ref, which):
        return ref.at[pl.ds(pl.multiple_of(which * 8, 8), 8)]

    for other in everyone:
        pltpu.make_async_remote_copy(
            src_ref=edge_flow.at[1, other], dst_ref=low_flow.at[rank], send_sem=send_sem.at[4],
            recv_sem=recv_sem.at[4], device_id=at(after, other), device_id_type=MESH,
        ).start()
    for other in everyone:
        pltpu.make_async_remote_copy(
            src_ref=edge_flow.at[0, other], dst_ref=high_flow.at[rank], send_sem=send_sem.at[3],
            recv_sem=recv_sem.at[3], device_id=at(before, other), device_id_type=MESH,
        ).start()
    for other in near:
        pltpu.make_async_remote_copy(
            src_ref=block(flow, other), dst_ref=block(flow_got, rank), send_sem=send_sem.at[5],
            recv_sem=recv_sem.at[5], device_id=at(space, other), device_id_type=MESH,
        ).start()
    mine = pl.ds(pl.multiple_of(rank * 8, 8), 8)
    flow_got[mine, :] = flow[mine, :]

    done += [
        total(edge_flow.at[0], high_flow, 3),
        total(edge_flow.at[1], low_flow, 4),
        total(flow.at[pl.ds(0, 8 * (GROUP - 1))], flow_got.at[pl.ds(0, 8 * (GROUP - 1))], 5),
    ]
    for d in done[3:]:
        d.wait_recv()
    owned = jnp.dot(
        spread, jnp.concatenate(split(flow_got[...]), axis=0), preferred_element_type=F32
    )
    low_sum, high_sum = low_flow[0], high_flow[0]
    for e in range(1, TILES):
        low_sum, high_sum = low_sum + low_flow[e], high_sum + high_flow[e]
    for w in range(TILES):
        piece = owned[2 * w : 2 * w + 2]
        if w == 0:
            piece = piece + low_sum
        if w == TILES - 1:
            piece = piece + high_sum
        out_ref[:, w * TILE : (w + 1) * TILE] = piece
    for d in done[:2] + done[3:]:
        d.wait_send()
    for other in hubs:
        to_hub(other).wait_send()

    @pl.when(core == 0)
    def _():
        to_hub(hub).wait_send()

    @pl.when(core == 1)
    def _():
        from_hub(rank - 4).wait_send()
        from_hub(rank).wait_send()


def per_device(coeffs, curl_tiles, pattern, region_ids, material_law, source):
    anywhere = pl.BlockSpec(memory_space=pltpu.HBM)
    total = pl.pallas_call(
        kernel,
        out_shape=pltpu.VMEM(source.shape, F32),
        in_specs=[anywhere] * 6,
        out_specs=pl.BlockSpec(memory_space=pltpu.VMEM),
        scratch_shapes=[
            pltpu.VMEM((2, TILES * TILE), BF16),
            pltpu.VMEM((LINKS, TILE, COMP), BF16),
            pltpu.VMEM((LINKS, TILES), jnp.int32),
            pltpu.VMEM((TILES,), jnp.int32),
            pltpu.VMEM((3, 4), F32),
            pltpu.VMEM((288, 256), BF16),
            pltpu.VMEM((TILES, 2 * LINKS, TILE), BF16),
            pltpu.VMEM((GROUP, 2 * LINKS, TILE), BF16),
            pltpu.VMEM((GROUP, 2, TILE), BF16),
            pltpu.VMEM((GROUP, 2, TILE), BF16),
            pltpu.VMEM((8, TILE), F32),
            pltpu.VMEM((GROUP * 8, TILE), F32),
            pltpu.VMEM((GROUP * 8, TILE), F32),
            pltpu.VMEM((2, GROUP, 2, TILE), F32),
            pltpu.VMEM((GROUP, 2, TILE), F32),
            pltpu.VMEM((GROUP, 2, TILE), F32),
            pltpu.SemaphoreType.DMA((6,)),
            pltpu.SemaphoreType.DMA((7,)),
            pltpu.SemaphoreType.DMA((7,)),
            pltpu.SemaphoreType.REGULAR,
            pltpu.VMEM((GROUP, 2, TILE), BF16),
        ],
        compiler_params=pltpu.CompilerParams(collective_id=0, has_side_effects=True),
        name="residual",
    )(coeffs, curl_tiles, pattern.T, region_ids, material_law, jnp.asarray(tables()))
    return total - source


def solution(mesh):
    placed = (
        P(("harm", "samp"), "space"),
        P("space", None, None, None),
        P("space", None),
        P("space"),
        P(),
        P(("harm", "samp"), "space"),
    )
    return jax.shard_map(
        per_device,
        mesh=mesh,
        in_specs=placed,
        out_specs=P(("harm", "samp"), "space"),
        check_vma=False,
    )
```

```python
import math

import jax
import jax.numpy as jnp
import ml_dtypes
import numpy as np
from jax import lax
from jax.experimental import pallas as pl
from jax.experimental.pallas import tpu as pltpu
from jax.sharding import PartitionSpec as P

SAMPLES = 64
HALF = SAMPLES // 2
PARTS = 32
GROUP = 16
HUBS = 8
OWN = 2
SPACE = 16
TILES = 16
LINKS = 4
TILE = 128
COMP = 3 * TILE
ROWS = OWN * LINKS * 2
WAVES = OWN * LINKS * HALF
MESH = pl.DeviceIdType.MESH
F32, BF16 = jnp.float32, jnp.bfloat16


def two_pieces(table):
    high = table.astype(ml_dtypes.bfloat16)
    low = (table - high.astype(np.float64)).astype(ml_dtypes.bfloat16)
    return high, low


def tables():
    t = np.arange(HALF)[:, None]
    q = np.arange(PARTS)[None, :]
    phase = ((2 * (q // 2) + 1) * t % SAMPLES) * (2.0 * math.pi / SAMPLES)
    transform = np.where(q % 2 == 0, np.cos(phase), np.sin(phase))
    by_rank = transform.reshape(HALF, GROUP, 2)
    main = np.zeros((OWN, LINKS, HALF, GROUP, OWN, LINKS, 2))
    for v in range(OWN):
        for k in range(LINKS):
            main[v, k, :, :, v, k, :] = by_rank
    main = main.reshape(WAVES, GROUP * ROWS)
    halo = np.zeros((HALF, GROUP * ROWS))
    halo[:, : 2 * PARTS] = np.tile(transform, (1, 2))
    back = (4.0 / SAMPLES) * by_rank.transpose(2, 1, 0).reshape(PARTS, HALF)
    back_high, back_low = two_pieces(back)
    back_row = np.zeros((PARTS, GROUP * ROWS), ml_dtypes.bfloat16)
    back_row[:, : 3 * HALF] = np.concatenate([back_high, back_low, back_high], axis=1)
    return np.concatenate([*two_pieces(main), *two_pieces(halo), back_row], axis=0)


def split(value):
    high = value.astype(BF16)
    return high, (value - high.astype(F32)).astype(BF16)


def kernel(
    coef_hbm, curl_hbm, pat_hbm, reg_hbm, law_hbm, tab_hbm, out_ref,
    coef, curl, pat, reg, law, tab, halo_tab, picks, got, firsts, low_got, high_got,
    flow, flow_got, edge_flow, low_flow, high_flow, local_sem, send_sem, recv_sem, ready,
):
    harm, space, samp = lax.axis_index("harm"), lax.axis_index("space"), lax.axis_index("samp")
    rank = harm * 4 + samp
    place = harm // 2 * 4 + samp
    core = lax.rem(harm, 2)
    after, before = lax.rem(space + 1, SPACE), lax.rem(space + SPACE - 1, SPACE)

    def rank_at(z, c):
        return (z // 4 * 2 + c) * 4 + lax.rem(z, 4)

    def at(group, other):
        return (other // 4, group, lax.rem(other, 4))

    far = [lax.rem(place + step, 8) for step in (4, 3, 5, 2, 6, 1, 7)]
    hubs = [(z, rank_at(z, 1)) for z in far]
    home = rank_at(place, 1)
    everyone = [rank_at(z, c) for z in far + [place] for c in (1 - core, core)]
    near = everyone[:-1]

    loads = [
        pltpu.make_async_copy(coef_hbm, coef, local_sem.at[0]),
        pltpu.make_async_copy(pat_hbm, pat, local_sem.at[1]),
        pltpu.make_async_copy(reg_hbm, reg, local_sem.at[2]),
        pltpu.make_async_copy(law_hbm, law, local_sem.at[3]),
        pltpu.make_async_copy(tab_hbm, tab, local_sem.at[4]),
        pltpu.make_async_copy(curl_hbm.at[pl.ds(OWN * place, OWN)], curl, local_sem.at[5]),
    ]
    for load in loads[:4]:
        load.start()
    barrier = pltpu.get_barrier_semaphore()

    @pl.when(core == 1)
    def _():
        for other in near:
            pl.semaphore_signal(barrier, inc=1, device_id=at(space, other), device_id_type=MESH)
        for other in everyone:
            pl.semaphore_signal(barrier, inc=1, device_id=at(before, other), device_id_type=MESH)
        for load in loads[4:]:
            load.start()

    loads[0].wait()
    loads[1].wait()
    pattern = pat[...].T
    rows = jnp.concatenate(
        [jnp.broadcast_to(pattern[e : e + 1, :], (2 * LINKS, LINKS)) for e in range(TILES)], axis=0
    )
    row = lax.broadcasted_iota(jnp.int32, (TILES * LINKS * 2, LINKS), 0)
    col = lax.broadcasted_iota(jnp.int32, (TILES * LINKS * 2, LINKS), 1)
    spot = jnp.sum(jnp.where(row // 2 % LINKS == col, rows, 0), axis=1, keepdims=True)
    row = lax.broadcasted_iota(jnp.int32, (TILES * LINKS * 2, TILES * 2), 0)
    col = lax.broadcasted_iota(jnp.int32, (TILES * LINKS * 2, TILES * 2), 1)
    hits = jnp.where((spot == col // 2 + 1) & (row % 2 == col % 2), 1.0, 0.0)
    own = coef[...].astype(F32)
    own = jnp.concatenate([own[:, w * TILE : (w + 1) * TILE] for w in range(TILES)], axis=0)
    picked = jnp.dot(hits.astype(BF16), own.astype(BF16), preferred_element_type=F32)
    picks[...] = picked.reshape(HUBS, ROWS, TILE).astype(BF16)
    spread = hits.T.astype(BF16)
    spread = jnp.concatenate([spread, spread], axis=1)

    loads[2].wait()
    loads[3].wait()
    links, laws = [], []
    for v in range(OWN):
        element = OWN * place + v
        own_row = lax.broadcasted_iota(jnp.int32, (TILES, LINKS), 0) == element
        links.append(jnp.sum(jnp.where(own_row, pattern, 0), axis=0, keepdims=True))
        region = reg[...].reshape(1, TILES)
        lane = lax.broadcasted_iota(jnp.int32, (1, TILES), 1)
        region = jnp.sum(jnp.where(lane == element, region, 0), axis=1, keepdims=True)
        lane = lax.broadcasted_iota(jnp.int32, (3, 4), 1)
        own_law = jnp.sum(jnp.where(lane == region, law[...], 0.0), axis=1, keepdims=True)
        laws.append((own_law[0:1], own_law[1:2], own_law[2:3]))

    @pl.when(core == 1)
    def _():
        loads[4].wait()
        lane = lax.broadcasted_iota(jnp.int32, (1, 2 * PARTS), 1)
        side = jnp.where(lane < PARTS, 0, TILES + 1)
        for piece in range(2):
            at_row = 2 * WAVES + piece * HALF
            plain = tab[at_row : at_row + HALF, 0 : 2 * PARTS].astype(F32)
            for v in range(OWN):
                for k in range(LINKS):
                    mask = jnp.where(links[v][:, k : k + 1] == side, 1.0, 0.0)
                    to_row = ((piece * OWN + v) * LINKS + k) * HALF
                    halo_tab[to_row : to_row + HALF, :] = (plain * mask).astype(BF16)
        loads[5].wait()

    def remote(src, dst, i, group, other):
        return pltpu.make_async_remote_copy(
            src_ref=src, dst_ref=dst, send_sem=send_sem.at[i], recv_sem=recv_sem.at[i],
            device_id=at(group, other), device_id_type=MESH,
        )

    pl.semaphore_wait(barrier, GROUP - core)

    @pl.when(core == 1)
    def _():
        pl.semaphore_signal(ready, inc=1, device_id=at(after, rank), device_id_type=MESH)

    first, last = coef.at[:, pl.ds(0, TILE)], coef.at[:, pl.ds((TILES - 1) * TILE, TILE)]
    sent_first = [remote(first, firsts.at[rank], 0, space, other) for _, other in hubs]
    sent_last = [remote(last, low_got.at[rank], 1, after, other) for _, other in hubs]
    sent_last.append(remote(last, low_got.at[rank], 1, after, home))
    sent_picks = [remote(picks.at[z], got.at[rank], 3, space, other) for z, other in hubs]
    home_first = remote(first, firsts.at[rank], 0, space, home)
    home_picks = remote(picks.at[place], got.at[rank], 3, space, home)
    for copy in sent_first:
        copy.start()

    @pl.when(core == 0)
    def _():
        home_first.start()

    for copy in sent_last + sent_picks:
        copy.start()

    @pl.when(core == 0)
    def _():
        home_picks.start()

    def block(ref, which):
        return ref.at[pl.ds(pl.multiple_of(which * ROWS, ROWS), ROWS)]

    @pl.when(core == 1)
    def _():
        firsts[rank] = coef[:, 0:TILE]
        got[rank] = picks[place]
        gathered = remote(
            firsts.at[pl.ds(0, GROUP - 1)], firsts.at[pl.ds(0, GROUP - 1)], 0, space, hubs[0][1]
        )
        gathered.wait_recv()
        pl.semaphore_wait(ready, 1)
        handed = remote(firsts, high_got, 2, before, rank)
        handed.start()
        picked = got.at[pl.ds(0, GROUP - 1)]
        remote(picked, picked, 3, space, hubs[0][1]).wait_recv()
        window = got[...].reshape(GROUP * ROWS, TILE)
        waves = jnp.dot(tab[0 : 2 * WAVES, :], window, preferred_element_type=F32)
        remote(low_got, low_got, 1, space, hubs[0][1]).wait_recv()
        handed.wait_recv()
        halo = [
            ref[...].astype(F32).reshape(PARTS, TILE).astype(BF16) for ref in (low_got, high_got)
        ]
        waves = waves + jnp.dot(
            halo_tab[...], jnp.concatenate(halo, axis=0), preferred_element_type=F32
        )
        waves = waves[:WAVES] + waves[WAVES:]
        fields, blocks = [], []
        for v in range(OWN):
            wave = jnp.concatenate(
                [
                    waves[(v * LINKS + k) * HALF : (v * LINKS + k + 1) * HALF]
                    for k in range(LINKS)
                ],
                axis=1,
            )
            blocks.append(curl[v].reshape(LINKS * TILE, COMP))
            density = jnp.dot(
                jnp.concatenate(split(wave), axis=0), blocks[v], preferred_element_type=F32
            )
            density = density[:HALF] + density[HALF:]
            comps = [density[:, c * TILE : (c + 1) * TILE] for c in range(3)]
            square = comps[0] * comps[0] + comps[1] * comps[1] + comps[2] * comps[2]
            base, knee, rise = laws[v]
            reluct = base + rise * square / (square + knee)
            fields += [reluct * c for c in comps]
        high, low = split(jnp.concatenate(fields, axis=1))
        back = tab[2 * WAVES + 2 * HALF : 2 * WAVES + 2 * HALF + PARTS, 0 : 3 * HALF]
        harmonic = jnp.dot(
            back, jnp.concatenate([high, high, low], axis=0), preferred_element_type=F32
        ).astype(BF16)
        edges = [jnp.zeros((PARTS, TILE), F32), jnp.zeros((PARTS, TILE), F32)]
        for v in range(OWN):
            contrib = lax.dot_general(
                harmonic[:, v * COMP : (v + 1) * COMP],
                blocks[v],
                (((1,), (1,)), ((), ())),
                preferred_element_type=F32,
            )
            for k in range(LINKS):
                tile = contrib[:, k * TILE : (k + 1) * TILE]
                for p in range(2):
                    flow[pl.ds((v * LINKS + k) * 2 + p, GROUP, stride=ROWS), :] = tile[
                        p * GROUP : (p + 1) * GROUP
                    ]
                for i, spot in enumerate((0, TILES + 1)):
                    edges[i] = edges[i] + jnp.where(links[v][:, k : k + 1] == spot, tile, 0.0)
        for i in range(2):
            for p in range(2):
                edge_flow[i, :, p, :] = edges[i][p * GROUP : (p + 1) * GROUP]

        to_after = [remote(edge_flow.at[1, o], low_flow.at[place], 4, after, o) for o in everyone]
        to_before = [remote(edge_flow.at[0, o], high_flow.at[place], 5, before, o) for o in everyone]
        to_group = [remote(block(flow, o), block(flow_got, place), 6, space, o) for o in near]
        for copy in to_after + to_group + to_before:
            copy.start()
        mine = pl.ds(pl.multiple_of(place * ROWS, ROWS), ROWS)
        flow_got[mine, :] = flow[pl.ds(pl.multiple_of(rank * ROWS, ROWS), ROWS), :]
        others = pl.ds(0, (HUBS - 1) * ROWS)
        remote(flow_got.at[others], flow_got.at[others], 6, space, hubs[0][1]).wait_recv()
        for copy in to_after + to_group + to_before:
            copy.wait_send()
        handed.wait_send()

    @pl.when(core == 0)
    def _():
        remote(flow_got, flow_got, 6, space, hubs[0][1]).wait_recv()

    remote(low_flow, low_flow, 4, space, hubs[0][1]).wait_recv()
    remote(high_flow, high_flow, 5, space, hubs[0][1]).wait_recv()
    owned = jnp.dot(
        spread, jnp.concatenate(split(flow_got[...]), axis=0), preferred_element_type=F32
    )
    low_sum, high_sum = low_flow[0], high_flow[0]
    for u in range(1, HUBS):
        low_sum, high_sum = low_sum + low_flow[u], high_sum + high_flow[u]
    for w in range(TILES):
        piece = owned[2 * w : 2 * w + 2]
        if w == 0:
            piece = piece + low_sum
        if w == TILES - 1:
            piece = piece + high_sum
        out_ref[:, w * TILE : (w + 1) * TILE] = piece
    for copy in sent_first + sent_last + sent_picks:
        copy.wait_send()

    @pl.when(core == 0)
    def _():
        home_first.wait_send()
        home_picks.wait_send()


def per_device(coeffs, curl_tiles, pattern, region_ids, material_law, source):
    anywhere = pl.BlockSpec(memory_space=pltpu.HBM)
    table = tables()
    total = pl.pallas_call(
        kernel,
        out_shape=pltpu.VMEM(source.shape, F32),
        in_specs=[anywhere] * 6,
        out_specs=pl.BlockSpec(memory_space=pltpu.VMEM),
        scratch_shapes=[
            pltpu.VMEM((2, TILES * TILE), BF16),
            pltpu.VMEM((OWN, LINKS, TILE, COMP), BF16),
            pltpu.VMEM((LINKS, TILES), jnp.int32),
            pltpu.VMEM((TILES,), jnp.int32),
            pltpu.VMEM((3, 4), F32),
            pltpu.VMEM(table.shape, BF16),
            pltpu.VMEM((2 * WAVES, 2 * PARTS), BF16),
            pltpu.VMEM((HUBS, ROWS, TILE), BF16),
            pltpu.VMEM((GROUP, ROWS, TILE), BF16),
            pltpu.VMEM((GROUP, 2, TILE), BF16),
            pltpu.VMEM((GROUP, 2, TILE), BF16),
            pltpu.VMEM((GROUP, 2, TILE), BF16),
            pltpu.VMEM((GROUP * ROWS, TILE), F32),
            pltpu.VMEM((HUBS * ROWS, TILE), F32),
            pltpu.VMEM((2, GROUP, 2, TILE), F32),
            pltpu.VMEM((HUBS, 2, TILE), F32),
            pltpu.VMEM((HUBS, 2, TILE), F32),
            pltpu.SemaphoreType.DMA((6,)),
            pltpu.SemaphoreType.DMA((7,)),
            pltpu.SemaphoreType.DMA((7,)),
            pltpu.SemaphoreType.REGULAR,
        ],
        compiler_params=pltpu.CompilerParams(collective_id=0, has_side_effects=True),
        name="residual",
    )(coeffs, curl_tiles, pattern.T, region_ids, material_law, jnp.asarray(table))
    return total - source


def solution(mesh):
    placed = (
        P(("harm", "samp"), "space"),
        P("space", None, None, None),
        P("space", None),
        P("space"),
        P(),
        P(("harm", "samp"), "space"),
    )
    return jax.shard_map(
        per_device,
        mesh=mesh,
        in_specs=placed,
        out_specs=P(("harm", "samp"), "space"),
        check_vma=False,
    )
```

```python
import math

import jax
import jax.numpy as jnp
import ml_dtypes
import numpy as np
from jax import lax
from jax.experimental import pallas as pl
from jax.experimental.pallas import tpu as pltpu
from jax.sharding import PartitionSpec as P

SAMPLES = 64
HALF = SAMPLES // 2
PARTS = 32
GROUP = 16
HUBS = 4
HUB = 4
OWN = 4
SPACE = 16
TILES = 16
LINKS = 4
TILE = 128
COMP = 3 * TILE
EDGE = LINKS * 2
ROWS = OWN * EDGE
WAVES = LINKS * HALF
MESH = pl.DeviceIdType.MESH
F32, BF16 = jnp.float32, jnp.bfloat16


def two_pieces(table):
    high = table.astype(ml_dtypes.bfloat16)
    low = (table - high.astype(np.float64)).astype(ml_dtypes.bfloat16)
    return high, low


def tables():
    t = np.arange(HALF)[:, None]
    q = np.arange(PARTS)[None, :]
    phase = ((2 * (q // 2) + 1) * t % SAMPLES) * (2.0 * math.pi / SAMPLES)
    transform = np.where(q % 2 == 0, np.cos(phase), np.sin(phase))
    by_rank = transform.reshape(HALF, GROUP, 2)
    main = np.zeros((LINKS, HALF, GROUP, LINKS, 2))
    for k in range(LINKS):
        main[k, :, :, k, :] = by_rank
    main = main.reshape(WAVES, TILE)
    halo = np.zeros((2, 2 * HALF, TILE), ml_dtypes.bfloat16)
    for side in range(2):
        halo[side, :, side * PARTS : (side + 1) * PARTS] = np.concatenate(two_pieces(transform))
    back = (4.0 / SAMPLES) * by_rank.transpose(2, 1, 0).reshape(PARTS, HALF)
    back_high, back_low = two_pieces(back)
    back_row = np.zeros((PARTS, TILE), ml_dtypes.bfloat16)
    back_row[:, : 3 * HALF] = np.concatenate([back_high, back_low, back_high], axis=1)
    return np.concatenate([*two_pieces(main), halo.reshape(4 * HALF, TILE), back_row], axis=0)


def split(value):
    high = value.astype(BF16)
    return high, (value - high.astype(F32)).astype(BF16)


def kernel(
    coef_hbm, curl_hbm, pat_hbm, reg_hbm, law_hbm, tab_hbm, out_ref,
    coef, curl, pat, reg, law, tab, picks, got, firsts, low_got, high_got,
    flow, flow_got, edge_flow, low_flow, high_flow, local_sem, send_sem, recv_sem, ready,
):
    harm, space, samp = lax.axis_index("harm"), lax.axis_index("space"), lax.axis_index("samp")
    rank = harm * 4 + samp
    is_hub = harm == 1
    after, before = lax.rem(space + 1, SPACE), lax.rem(space + SPACE - 1, SPACE)

    def at(group, other):
        if isinstance(other, int):
            return (other // 4, group, other % 4)
        return (other // 4, group, lax.rem(other, 4))

    home = HUB + samp
    hubs = [HUB + lax.rem(samp + d, HUBS) for d in range(1, HUBS)]
    launched = [(z // 4 * 2 + c) * 4 + z % 4 for z in range(8) for c in (1, 0)]
    plain = [other for other in launched if other // 4 != 1]

    loads = [
        pltpu.make_async_copy(coef_hbm, coef, local_sem.at[0]),
        pltpu.make_async_copy(pat_hbm, pat, local_sem.at[1]),
        pltpu.make_async_copy(reg_hbm, reg, local_sem.at[2]),
        pltpu.make_async_copy(law_hbm, law, local_sem.at[3]),
        pltpu.make_async_copy(tab_hbm, tab, local_sem.at[4]),
        pltpu.make_async_copy(curl_hbm.at[pl.ds(OWN * samp, OWN)], curl, local_sem.at[5]),
    ]
    for load in loads[:4]:
        load.start()
    barrier = pltpu.get_barrier_semaphore()

    @pl.when(is_hub)
    def _():
        for group, others in ((space, hubs), (before, [*hubs, home]), (space, plain), (before, plain)):
            for other in others:
                pl.semaphore_signal(barrier, inc=1, device_id=at(group, other), device_id_type=MESH)
        for load in loads[4:]:
            load.start()

    loads[0].wait()
    loads[1].wait()
    pattern = pat[...].T
    rows = jnp.concatenate(
        [jnp.broadcast_to(pattern[e : e + 1, :], (2 * LINKS, LINKS)) for e in range(TILES)], axis=0
    )
    row = lax.broadcasted_iota(jnp.int32, (TILES * LINKS * 2, LINKS), 0)
    col = lax.broadcasted_iota(jnp.int32, (TILES * LINKS * 2, LINKS), 1)
    spot = jnp.sum(jnp.where(row // 2 % LINKS == col, rows, 0), axis=1, keepdims=True)
    row = lax.broadcasted_iota(jnp.int32, (TILES * LINKS * 2, TILES * 2), 0)
    col = lax.broadcasted_iota(jnp.int32, (TILES * LINKS * 2, TILES * 2), 1)
    hits = jnp.where((spot == col // 2 + 1) & (row % 2 == col % 2), 1.0, 0.0)
    own = coef[...].astype(F32)
    own = jnp.concatenate([own[:, w * TILE : (w + 1) * TILE] for w in range(TILES)], axis=0)
    picked = jnp.dot(hits.astype(BF16), own.astype(BF16), preferred_element_type=F32)
    picks[...] = picked.reshape(HUBS, OWN, EDGE, TILE).astype(BF16)
    spread = hits.T.astype(BF16)
    spread = jnp.concatenate([spread, spread], axis=1)

    loads[2].wait()
    loads[3].wait()
    links, laws = [], []
    for v in range(OWN):
        element = OWN * samp + v
        own_row = lax.broadcasted_iota(jnp.int32, (TILES, LINKS), 0) == element
        links.append(jnp.sum(jnp.where(own_row, pattern, 0), axis=0, keepdims=True))
        region = reg[...].reshape(1, TILES)
        lane = lax.broadcasted_iota(jnp.int32, (1, TILES), 1)
        region = jnp.sum(jnp.where(lane == element, region, 0), axis=1, keepdims=True)
        lane = lax.broadcasted_iota(jnp.int32, (3, 4), 1)
        own_law = jnp.sum(jnp.where(lane == region, law[...], 0.0), axis=1, keepdims=True)
        laws.append((own_law[0:1], own_law[1:2], own_law[2:3]))

    @pl.when(is_hub)
    def _():
        loads[4].wait()
        loads[5].wait()

    def remote(src, dst, i, group, other):
        return pltpu.make_async_remote_copy(
            src_ref=src, dst_ref=dst, send_sem=send_sem.at[i], recv_sem=recv_sem.at[i],
            device_id=at(group, other), device_id_type=MESH,
        )

    pl.semaphore_wait(barrier, jnp.where(is_hub, 2 * HUBS - 1, 2 * HUBS))

    @pl.when(is_hub)
    def _():
        pl.semaphore_signal(ready, inc=1, device_id=at(after, rank), device_id_type=MESH)

    first, last = coef.at[:, pl.ds(0, TILE)], coef.at[:, pl.ds((TILES - 1) * TILE, TILE)]
    sent_first = [remote(first, firsts.at[rank], 0, space, other) for other in hubs]
    sent_last = [remote(last, low_got.at[rank], 1, after, other) for other in [home, *hubs]]
    sent_picks = [remote(picks.at[other - HUB], got.at[rank], 3, space, other) for other in hubs]
    home_first = remote(first, firsts.at[rank], 0, space, home)
    home_picks = remote(picks.at[samp], got.at[rank], 3, space, home)

    @pl.when(jnp.logical_not(is_hub))
    def _():
        home_first.start()

    for copy in sent_first + sent_last:
        copy.start()

    @pl.when(jnp.logical_not(is_hub))
    def _():
        home_picks.start()

    for copy in sent_picks:
        copy.start()

    def block(ref, which):
        start = which * ROWS if isinstance(which, int) else pl.multiple_of(which * ROWS, ROWS)
        return ref.at[pl.ds(start, ROWS)]

    @pl.when(is_hub)
    def _():
        firsts[rank] = coef[:, 0:TILE]
        got[rank] = picks[samp]
        gathered = firsts.at[pl.ds(0, GROUP - 1)]
        remote(gathered, gathered, 0, space, hubs[0]).wait_recv()
        pl.semaphore_wait(ready, 1)
        handed = remote(firsts, high_got, 2, before, rank)
        handed.start()
        picked = got.at[pl.ds(0, GROUP - 1)]
        remote(picked, picked, 3, space, hubs[0]).wait_recv()
        waves = []
        for v in range(OWN):
            window = got[:, v].reshape(GROUP * EDGE, TILE)
            wave = jnp.dot(tab[0 : 2 * WAVES, :], window, preferred_element_type=F32)
            waves.append(wave[:WAVES] + wave[WAVES:])
        remote(low_got, low_got, 1, space, hubs[0]).wait_recv()
        handed.wait_recv()
        halo = [
            ref[...].astype(F32).reshape(PARTS, TILE).astype(BF16) for ref in (low_got, high_got)
        ]
        halo = jnp.dot(
            tab[2 * WAVES : 2 * WAVES + 4 * HALF, 0 : 2 * PARTS],
            jnp.concatenate(halo, axis=0),
            preferred_element_type=F32,
        )
        halo = [halo[2 * i * HALF :][:HALF] + halo[(2 * i + 1) * HALF :][:HALF] for i in range(2)]
        back = tab[2 * WAVES + 4 * HALF : 2 * WAVES + 4 * HALF + PARTS, 0 : 3 * HALF]
        edges = [jnp.zeros((PARTS, TILE), F32), jnp.zeros((PARTS, TILE), F32)]
        for v in range(OWN):
            wave = []
            for k in range(LINKS):
                piece = waves[v][k * HALF : (k + 1) * HALF]
                for i, spot in enumerate((0, TILES + 1)):
                    piece = piece + jnp.where(links[v][:, k : k + 1] == spot, halo[i], 0.0)
                wave.append(piece)
            blocks = curl[v].reshape(LINKS * TILE, COMP)
            density = jnp.dot(
                jnp.concatenate(split(jnp.concatenate(wave, axis=1)), axis=0),
                blocks,
                preferred_element_type=F32,
            )
            density = density[:HALF] + density[HALF:]
            comps = [density[:, c * TILE : (c + 1) * TILE] for c in range(3)]
            square = comps[0] * comps[0] + comps[1] * comps[1] + comps[2] * comps[2]
            base, knee, rise = laws[v]
            reluct = base + rise * square / (square + knee)
            high, low = split(jnp.concatenate([reluct * c for c in comps], axis=1))
            harmonic = jnp.dot(
                back, jnp.concatenate([high, high, low], axis=0), preferred_element_type=F32
            )
            contrib = lax.dot_general(
                harmonic.astype(BF16), blocks, (((1,), (1,)), ((), ())), preferred_element_type=F32
            )
            for k in range(LINKS):
                tile = contrib[:, k * TILE : (k + 1) * TILE]
                for p in range(2):
                    flow[pl.ds(v * EDGE + 2 * k + p, GROUP, stride=ROWS), :] = tile[
                        p * GROUP : (p + 1) * GROUP
                    ]
                for i, spot in enumerate((0, TILES + 1)):
                    edges[i] = edges[i] + jnp.where(links[v][:, k : k + 1] == spot, tile, 0.0)
        for i in range(2):
            for p in range(2):
                edge_flow[i, :, p, :] = edges[i][p * GROUP : (p + 1) * GROUP]

        to_after = [remote(edge_flow.at[1, o], low_flow.at[samp], 4, after, o) for o in launched]
        to_before = [remote(edge_flow.at[0, o], high_flow.at[samp], 5, before, o) for o in launched]
        to_group = [remote(block(flow, o), block(flow_got, samp), 6, space, o) for o in launched]
        for other, *copies in zip(launched, to_after, to_group, to_before):
            copies[0].start()

            @pl.when(rank != other)
            def _():
                copies[1].start()

            copies[2].start()
        mine = pl.ds(pl.multiple_of(samp * ROWS, ROWS), ROWS)
        flow_got[mine, :] = flow[pl.ds(pl.multiple_of(rank * ROWS, ROWS), ROWS), :]
        others = pl.ds(0, (HUBS - 1) * ROWS)
        remote(flow_got.at[others], flow_got.at[others], 6, space, hubs[0]).wait_recv()

    @pl.when(jnp.logical_not(is_hub))
    def _():
        remote(flow_got, flow_got, 6, space, home).wait_recv()

    remote(low_flow, low_flow, 4, after, home).wait_recv()
    remote(high_flow, high_flow, 5, after, home).wait_recv()
    owned = jnp.dot(
        spread, jnp.concatenate(split(flow_got[...]), axis=0), preferred_element_type=F32
    )
    low_sum, high_sum = low_flow[0], high_flow[0]
    for u in range(1, HUBS):
        low_sum, high_sum = low_sum + low_flow[u], high_sum + high_flow[u]
    for w in range(TILES):
        piece = owned[2 * w : 2 * w + 2]
        if w == 0:
            piece = piece + low_sum
        if w == TILES - 1:
            piece = piece + high_sum
        out_ref[:, w * TILE : (w + 1) * TILE] = piece
    for copy in sent_first + sent_last + sent_picks:
        copy.wait_send()

    @pl.when(jnp.logical_not(is_hub))
    def _():
        home_first.wait_send()
        home_picks.wait_send()

    @pl.when(is_hub)
    def _():
        others = pl.ds(0, (GROUP - 1) * ROWS)
        remote(firsts, high_got, 2, before, rank).wait_send()
        remote(edge_flow.at[1], edge_flow.at[1], 4, after, home).wait_send()
        remote(edge_flow.at[0], edge_flow.at[0], 5, after, home).wait_send()
        remote(flow.at[others], flow.at[others], 6, after, home).wait_send()


def per_device(coeffs, curl_tiles, pattern, region_ids, material_law, source):
    anywhere = pl.BlockSpec(memory_space=pltpu.HBM)
    table = tables()
    total = pl.pallas_call(
        kernel,
        out_shape=pltpu.VMEM(source.shape, F32),
        in_specs=[anywhere] * 6,
        out_specs=pl.BlockSpec(memory_space=pltpu.VMEM),
        scratch_shapes=[
            pltpu.VMEM((2, TILES * TILE), BF16),
            pltpu.VMEM((OWN, LINKS, TILE, COMP), BF16),
            pltpu.VMEM((LINKS, TILES), jnp.int32),
            pltpu.VMEM((TILES,), jnp.int32),
            pltpu.VMEM((3, 4), F32),
            pltpu.VMEM(table.shape, BF16),
            pltpu.VMEM((HUBS, OWN, EDGE, TILE), BF16),
            pltpu.VMEM((GROUP, OWN, EDGE, TILE), BF16),
            pltpu.VMEM((GROUP, 2, TILE), BF16),
            pltpu.VMEM((GROUP, 2, TILE), BF16),
            pltpu.VMEM((GROUP, 2, TILE), BF16),
            pltpu.VMEM((GROUP * ROWS, TILE), F32),
            pltpu.VMEM((HUBS * ROWS, TILE), F32),
            pltpu.VMEM((2, GROUP, 2, TILE), F32),
            pltpu.VMEM((HUBS, 2, TILE), F32),
            pltpu.VMEM((HUBS, 2, TILE), F32),
            pltpu.SemaphoreType.DMA((6,)),
            pltpu.SemaphoreType.DMA((7,)),
            pltpu.SemaphoreType.DMA((7,)),
            pltpu.SemaphoreType.REGULAR,
        ],
        compiler_params=pltpu.CompilerParams(collective_id=0, has_side_effects=True),
        name="residual",
    )(coeffs, curl_tiles, pattern.T, region_ids, material_law, jnp.asarray(table))
    return total - source


def solution(mesh):
    placed = (
        P(("harm", "samp"), "space"),
        P("space", None, None, None),
        P("space", None),
        P("space"),
        P(),
        P(("harm", "samp"), "space"),
    )
    return jax.shard_map(
        per_device,
        mesh=mesh,
        in_specs=placed,
        out_specs=P(("harm", "samp"), "space"),
        check_vma=False,
    )
```

```python
import math

import jax
import jax.numpy as jnp
import ml_dtypes
import numpy as np
from jax import lax
from jax.experimental import pallas as pl
from jax.experimental.pallas import tpu as pltpu
from jax.sharding import PartitionSpec as P

SAMPLES = 64
HALF = SAMPLES // 2
PARTS = 32
GROUP = 16
HUBS = 4
HUB = 4
OWN = 4
SPACE = 16
TILES = 16
LINKS = 4
TILE = 128
COMP = 3 * TILE
EDGE = LINKS * 2
ROWS = OWN * EDGE
WAVES = LINKS * HALF
MESH = pl.DeviceIdType.MESH
F32, BF16 = jnp.float32, jnp.bfloat16


def two_pieces(table):
    high = table.astype(ml_dtypes.bfloat16)
    low = (table - high.astype(np.float64)).astype(ml_dtypes.bfloat16)
    return high, low


def tables():
    t = np.arange(HALF)[:, None]
    q = np.arange(PARTS)[None, :]
    phase = ((2 * (q // 2) + 1) * t % SAMPLES) * (2.0 * math.pi / SAMPLES)
    transform = np.where(q % 2 == 0, np.cos(phase), np.sin(phase))
    by_rank = transform.reshape(HALF, GROUP, 2)
    main = np.zeros((LINKS, HALF, GROUP, LINKS, 2))
    for k in range(LINKS):
        main[k, :, :, k, :] = by_rank
    main = np.concatenate(two_pieces(main.reshape(WAVES, TILE)), axis=1)
    halo = np.zeros((2, HALF, 2, 2, PARTS), ml_dtypes.bfloat16)
    for piece, part in enumerate(two_pieces(transform)):
        for side in range(2):
            halo[side, :, piece, side] = part
    halo = np.pad(halo.reshape(2 * HALF, TILE), ((0, 0), (0, TILE)))
    back = (4.0 / SAMPLES) * by_rank.transpose(2, 1, 0).reshape(PARTS, HALF)
    back_high, back_low = two_pieces(back)
    back_row = np.zeros((PARTS, 2 * TILE), ml_dtypes.bfloat16)
    back_row[:, : 3 * HALF] = np.concatenate([back_high, back_low, back_high], axis=1)
    return np.concatenate([main, halo, back_row], axis=0)


def split(value):
    high = value.astype(BF16)
    return high, (value - high.astype(F32)).astype(BF16)


def kernel(
    coef_hbm, curl_hbm, pat_hbm, reg_hbm, law_hbm, tab_hbm, out_ref,
    coef, curl, pat, reg, law, tab, picks, got, firsts, low_got, high_got,
    flow, flow_got, edge_flow, low_flow, high_flow, local_sem, send_sem, recv_sem, ready, curl_t,
):
    harm, space, samp = lax.axis_index("harm"), lax.axis_index("space"), lax.axis_index("samp")
    rank = harm * 4 + samp
    is_hub = harm == 1
    after, before = lax.rem(space + 1, SPACE), lax.rem(space + SPACE - 1, SPACE)

    def at(group, other):
        if isinstance(other, int):
            return (other // 4, group, other % 4)
        return (other // 4, group, lax.rem(other, 4))

    home = HUB + samp
    hubs = [HUB + lax.rem(samp + d, HUBS) for d in range(1, HUBS)]
    launched = [(z // 4 * 2 + c) * 4 + z % 4 for z in range(8) for c in (1, 0)]
    plain = [other for other in launched if other // 4 != 1]

    loads = [
        pltpu.make_async_copy(coef_hbm, coef, local_sem.at[0]),
        pltpu.make_async_copy(pat_hbm, pat, local_sem.at[1]),
        pltpu.make_async_copy(reg_hbm, reg, local_sem.at[2]),
        pltpu.make_async_copy(law_hbm, law, local_sem.at[3]),
        pltpu.make_async_copy(tab_hbm, tab, local_sem.at[4]),
        pltpu.make_async_copy(curl_hbm.at[pl.ds(OWN * samp, OWN)], curl, local_sem.at[5]),
    ]
    barrier = pltpu.get_barrier_semaphore()

    @pl.when(is_hub)
    def _():
        def greet(group, other):
            pl.semaphore_signal(barrier, inc=1, device_id=at(group, other), device_id_type=MESH)

        for other in hubs:
            greet(space, other)
            greet(before, other)
        for other in reversed(plain):
            greet(space, other)
            greet(before, other)
        greet(before, home)
        for load in loads[4:]:
            load.start()

    for load in loads[:4]:
        load.start()

    loads[0].wait()
    loads[1].wait()
    pattern = pat[...].T
    rows = jnp.concatenate(
        [jnp.broadcast_to(pattern[e : e + 1, :], (2 * LINKS, LINKS)) for e in range(TILES)], axis=0
    )
    row = lax.broadcasted_iota(jnp.int32, (TILES * LINKS * 2, LINKS), 0)
    col = lax.broadcasted_iota(jnp.int32, (TILES * LINKS * 2, LINKS), 1)
    spot = jnp.sum(jnp.where(row // 2 % LINKS == col, rows, 0), axis=1, keepdims=True)
    row = lax.broadcasted_iota(jnp.int32, (TILES * LINKS * 2, TILES * 2), 0)
    col = lax.broadcasted_iota(jnp.int32, (TILES * LINKS * 2, TILES * 2), 1)
    hits = jnp.where((spot == col // 2 + 1) & (row % 2 == col % 2), 1.0, 0.0)
    own = coef[...].astype(F32)
    own = jnp.concatenate([own[:, w * TILE : (w + 1) * TILE] for w in range(TILES)], axis=0)
    picked = jnp.dot(hits.astype(BF16), own.astype(BF16), preferred_element_type=F32)
    picks[...] = picked.reshape(HUBS, OWN, EDGE, TILE).astype(BF16)
    spread = hits.T.astype(BF16)
    spread = jnp.concatenate([spread, spread], axis=1)

    loads[2].wait()
    loads[3].wait()
    links, laws = [], []
    for v in range(OWN):
        element = OWN * samp + v
        own_row = lax.broadcasted_iota(jnp.int32, (TILES, LINKS), 0) == element
        links.append(jnp.sum(jnp.where(own_row, pattern, 0), axis=0, keepdims=True))
        region = reg[...].reshape(1, TILES)
        lane = lax.broadcasted_iota(jnp.int32, (1, TILES), 1)
        region = jnp.sum(jnp.where(lane == element, region, 0), axis=1, keepdims=True)
        lane = lax.broadcasted_iota(jnp.int32, (3, 4), 1)
        own_law = jnp.sum(jnp.where(lane == region, law[...], 0.0), axis=1, keepdims=True)
        laws.append((own_law[0:1], own_law[1:2], own_law[2:3]))

    @pl.when(is_hub)
    def _():
        loads[4].wait()
        loads[5].wait()

    def remote(src, dst, i, group, other):
        return pltpu.make_async_remote_copy(
            src_ref=src, dst_ref=dst, send_sem=send_sem.at[i], recv_sem=recv_sem.at[i],
            device_id=at(group, other), device_id_type=MESH,
        )

    pl.semaphore_wait(barrier, jnp.where(is_hub, 2 * HUBS - 1, 2 * HUBS))

    @pl.when(is_hub)
    def _():
        pl.semaphore_signal(ready, inc=1, device_id=at(after, rank), device_id_type=MESH)

    first, last = coef.at[:, pl.ds(0, TILE)], coef.at[:, pl.ds((TILES - 1) * TILE, TILE)]
    sent_first = [remote(first, firsts.at[rank], 0, space, other) for other in hubs]
    sent_last = [remote(last, low_got.at[rank], 1, after, other) for other in [home, *hubs]]
    sent_picks = [remote(picks.at[other - HUB], got.at[rank], 3, space, other) for other in hubs]
    home_first = remote(first, firsts.at[rank], 0, space, home)
    home_picks = remote(picks.at[samp], got.at[rank], 3, space, home)

    @pl.when(jnp.logical_not(is_hub))
    def _():
        home_first.start()

    for copy in sent_first + sent_last:
        copy.start()

    @pl.when(jnp.logical_not(is_hub))
    def _():
        home_picks.start()

    for copy in sent_picks:
        copy.start()

    def block(ref, which):
        start = which * ROWS if isinstance(which, int) else pl.multiple_of(which * ROWS, ROWS)
        return ref.at[pl.ds(start, ROWS)]

    @pl.when(is_hub)
    def _():
        firsts[rank] = coef[:, 0:TILE]
        got[rank] = picks[samp]
        for v in range(OWN):
            curl_t[v] = curl[v].reshape(LINKS * TILE, COMP).T
        gathered = firsts.at[pl.ds(0, GROUP - 1)]
        remote(gathered, gathered, 0, space, hubs[0]).wait_recv()
        pl.semaphore_wait(ready, 1)
        handed = remote(firsts, high_got, 2, before, rank)
        handed.start()
        picked = got.at[pl.ds(0, GROUP - 1)]
        remote(picked, picked, 3, space, hubs[0]).wait_recv()
        windows = jnp.concatenate(
            [got[:, v].reshape(GROUP * EDGE, TILE) for v in range(OWN)], axis=1
        )
        waves = jnp.dot(
            tab[0:WAVES, :],
            jnp.concatenate([windows, windows], axis=0),
            preferred_element_type=F32,
        )
        remote(low_got, low_got, 1, space, hubs[0]).wait_recv()
        handed.wait_recv()
        halo = [
            ref[...].astype(F32).reshape(PARTS, TILE).astype(BF16) for ref in (low_got, high_got)
        ]
        halo = jnp.dot(
            tab[WAVES : WAVES + 2 * HALF, 0:TILE],
            jnp.concatenate([*halo, *halo], axis=0),
            preferred_element_type=F32,
        )
        halo = [halo[:HALF], halo[HALF:]]
        back = tab[WAVES + 2 * HALF : WAVES + 2 * HALF + PARTS, 0 : 3 * HALF]
        contribs = []
        edges = [jnp.zeros((PARTS, TILE), F32), jnp.zeros((PARTS, TILE), F32)]
        for v in range(OWN):
            wave = []
            for k in range(LINKS):
                piece = waves[k * HALF : (k + 1) * HALF, v * TILE : (v + 1) * TILE]
                for i, spot in enumerate((0, TILES + 1)):
                    piece = piece + jnp.where(links[v][:, k : k + 1] == spot, halo[i], 0.0)
                wave.append(piece)
            blocks = curl[v].reshape(LINKS * TILE, COMP)
            density = jnp.dot(
                jnp.concatenate(split(jnp.concatenate(wave, axis=1)), axis=0),
                blocks,
                preferred_element_type=F32,
            )
            density = density[:HALF] + density[HALF:]
            comps = [density[:, c * TILE : (c + 1) * TILE] for c in range(3)]
            square = comps[0] * comps[0] + comps[1] * comps[1] + comps[2] * comps[2]
            base, knee, rise = laws[v]
            reluct = base + rise * square / (square + knee)
            high, low = split(jnp.concatenate([reluct * c for c in comps], axis=1))
            harmonic = jnp.dot(
                back, jnp.concatenate([high, high, low], axis=0), preferred_element_type=F32
            )
            contrib = jnp.dot(
                harmonic.astype(BF16), curl_t[v], preferred_element_type=F32
            )
            contribs.append(contrib)
            for k in range(LINKS):
                tile = contrib[:, k * TILE : (k + 1) * TILE]
                for i, spot in enumerate((0, TILES + 1)):
                    edges[i] = edges[i] + jnp.where(links[v][:, k : k + 1] == spot, tile, 0.0)
        for i in range(2):
            for p in range(2):
                edge_flow[i, :, p, :] = edges[i][p * GROUP : (p + 1) * GROUP]

        to_after = [remote(edge_flow.at[1, o], low_flow.at[samp], 4, after, o) for o in launched]
        to_before = [remote(edge_flow.at[0, o], high_flow.at[samp], 5, before, o) for o in launched]
        to_group = [remote(block(flow, o), block(flow_got, samp), 6, space, o) for o in launched]
        for copy in to_after:
            copy.start()
        for v in range(OWN):
            for k in range(LINKS):
                for p in range(2):
                    flow[pl.ds(v * EDGE + 2 * k + p, GROUP, stride=ROWS), :] = contribs[v][
                        p * GROUP : (p + 1) * GROUP, k * TILE : (k + 1) * TILE
                    ]
        for other, *copies in zip(launched, to_group, to_before):

            @pl.when(rank != other)
            def _():
                copies[0].start()

            copies[1].start()
        mine = pl.ds(pl.multiple_of(samp * ROWS, ROWS), ROWS)
        flow_got[mine, :] = flow[pl.ds(pl.multiple_of(rank * ROWS, ROWS), ROWS), :]
        others = pl.ds(0, (HUBS - 1) * ROWS)
        remote(flow_got.at[others], flow_got.at[others], 6, space, hubs[0]).wait_recv()

    @pl.when(jnp.logical_not(is_hub))
    def _():
        remote(flow_got, flow_got, 6, space, home).wait_recv()

    remote(low_flow, low_flow, 4, after, home).wait_recv()
    remote(high_flow, high_flow, 5, after, home).wait_recv()
    owned = jnp.dot(
        spread, jnp.concatenate(split(flow_got[...]), axis=0), preferred_element_type=F32
    )
    low_sum, high_sum = low_flow[0], high_flow[0]
    for u in range(1, HUBS):
        low_sum, high_sum = low_sum + low_flow[u], high_sum + high_flow[u]
    for w in range(TILES):
        piece = owned[2 * w : 2 * w + 2]
        if w == 0:
            piece = piece + low_sum
        if w == TILES - 1:
            piece = piece + high_sum
        out_ref[:, w * TILE : (w + 1) * TILE] = piece
    for copy in sent_first + sent_last + sent_picks:
        copy.wait_send()

    @pl.when(jnp.logical_not(is_hub))
    def _():
        home_first.wait_send()
        home_picks.wait_send()

    @pl.when(is_hub)
    def _():
        others = pl.ds(0, (GROUP - 1) * ROWS)
        remote(firsts, high_got, 2, before, rank).wait_send()
        remote(edge_flow.at[1], edge_flow.at[1], 4, after, home).wait_send()
        remote(edge_flow.at[0], edge_flow.at[0], 5, after, home).wait_send()
        remote(flow.at[others], flow.at[others], 6, after, home).wait_send()


def per_device(coeffs, curl_tiles, pattern, region_ids, material_law, source):
    anywhere = pl.BlockSpec(memory_space=pltpu.HBM)
    table = tables()
    total = pl.pallas_call(
        kernel,
        out_shape=pltpu.VMEM(source.shape, F32),
        in_specs=[anywhere] * 6,
        out_specs=pl.BlockSpec(memory_space=pltpu.VMEM),
        scratch_shapes=[
            pltpu.VMEM((2, TILES * TILE), BF16),
            pltpu.VMEM((OWN, LINKS, TILE, COMP), BF16),
            pltpu.VMEM((LINKS, TILES), jnp.int32),
            pltpu.VMEM((TILES,), jnp.int32),
            pltpu.VMEM((3, 4), F32),
            pltpu.VMEM(table.shape, BF16),
            pltpu.VMEM((HUBS, OWN, EDGE, TILE), BF16),
            pltpu.VMEM((GROUP, OWN, EDGE, TILE), BF16),
            pltpu.VMEM((GROUP, 2, TILE), BF16),
            pltpu.VMEM((GROUP, 2, TILE), BF16),
            pltpu.VMEM((GROUP, 2, TILE), BF16),
            pltpu.VMEM((GROUP * ROWS, TILE), F32),
            pltpu.VMEM((HUBS * ROWS, TILE), F32),
            pltpu.VMEM((2, GROUP, 2, TILE), F32),
            pltpu.VMEM((HUBS, 2, TILE), F32),
            pltpu.VMEM((HUBS, 2, TILE), F32),
            pltpu.SemaphoreType.DMA((6,)),
            pltpu.SemaphoreType.DMA((7,)),
            pltpu.SemaphoreType.DMA((7,)),
            pltpu.SemaphoreType.REGULAR,
            pltpu.VMEM((OWN, COMP, LINKS * TILE), BF16),
        ],
        compiler_params=pltpu.CompilerParams(collective_id=0, has_side_effects=True),
        name="residual",
    )(coeffs, curl_tiles, pattern.T, region_ids, material_law, jnp.asarray(table))
    return total - source


def solution(mesh):
    placed = (
        P(("harm", "samp"), "space"),
        P("space", None, None, None),
        P("space", None),
        P("space"),
        P(),
        P(("harm", "samp"), "space"),
    )
    return jax.shard_map(
        per_device,
        mesh=mesh,
        in_specs=placed,
        out_specs=P(("harm", "samp"), "space"),
        check_vma=False,
    )
```

```python
import math

import jax
import jax.numpy as jnp
import ml_dtypes
import numpy as np
from jax import lax
from jax.experimental import pallas as pl
from jax.experimental.pallas import tpu as pltpu
from jax.sharding import PartitionSpec as P

SAMPLES = 64
HALF = SAMPLES // 2
PARTS = 32
GROUP = 16
HUBS = 4
HUB = 4
OWN = 4
SPACE = 16
TILES = 16
LINKS = 4
TILE = 128
COMP = 3 * TILE
EDGE = LINKS * 2
ROWS = OWN * EDGE
WAVES = LINKS * HALF
MESH = pl.DeviceIdType.MESH
F32, BF16 = jnp.float32, jnp.bfloat16


def two_pieces(table):
    high = table.astype(ml_dtypes.bfloat16)
    low = (table - high.astype(np.float64)).astype(ml_dtypes.bfloat16)
    return high, low


def tables():
    t = np.arange(HALF)[:, None]
    q = np.arange(PARTS)[None, :]
    phase = ((2 * (q // 2) + 1) * t % SAMPLES) * (2.0 * math.pi / SAMPLES)
    transform = np.where(q % 2 == 0, np.cos(phase), np.sin(phase))
    by_rank = transform.reshape(HALF, GROUP, 2)
    main = np.zeros((LINKS, HALF, GROUP, LINKS, 2))
    for k in range(LINKS):
        main[k, :, :, k, :] = by_rank
    main = np.concatenate(two_pieces(main.reshape(WAVES, TILE)), axis=1)
    halo = np.zeros((2, HALF, 2, 2, PARTS), ml_dtypes.bfloat16)
    for piece, part in enumerate(two_pieces(transform)):
        for side in range(2):
            halo[side, :, piece, side] = part
    halo = np.pad(halo.reshape(2 * HALF, TILE), ((0, 0), (0, TILE)))
    back = (4.0 / SAMPLES) * by_rank.transpose(2, 1, 0).reshape(PARTS, HALF)
    back_high, back_low = two_pieces(back)
    back_row = np.zeros((PARTS, 2 * TILE), ml_dtypes.bfloat16)
    back_row[:, : 3 * HALF] = np.concatenate([back_high, back_low, back_high], axis=1)
    return np.concatenate([main, halo, back_row], axis=0)


def split(value):
    high = value.astype(BF16)
    return high, (value - high.astype(F32)).astype(BF16)


def kernel(
    coef_hbm, curl_hbm, pat_hbm, reg_hbm, law_hbm, tab_hbm, out_ref,
    coef, curl, pat, reg, law, tab, picks, got, firsts, low_got, high_got,
    flow, flow_got, edge_flow, low_flow, high_flow, local_sem, send_sem, recv_sem, ready, curl_t,
):
    harm, space, samp = lax.axis_index("harm"), lax.axis_index("space"), lax.axis_index("samp")
    rank = harm * 4 + samp
    is_hub = harm == 1
    after, before = lax.rem(space + 1, SPACE), lax.rem(space + SPACE - 1, SPACE)

    def at(group, other):
        if isinstance(other, int):
            return (other // 4, group, other % 4)
        return (other // 4, group, lax.rem(other, 4))

    home = HUB + samp
    hubs = [HUB + lax.rem(samp + d, HUBS) for d in range(1, HUBS)]
    launched = [(z // 4 * 2 + c) * 4 + z % 4 for z in range(8) for c in (1, 0)]
    plain = [other for other in launched if other // 4 != 1]

    loads = [
        pltpu.make_async_copy(coef_hbm, coef, local_sem.at[0]),
        pltpu.make_async_copy(pat_hbm, pat, local_sem.at[1]),
        pltpu.make_async_copy(reg_hbm, reg, local_sem.at[2]),
        pltpu.make_async_copy(law_hbm, law, local_sem.at[3]),
        pltpu.make_async_copy(tab_hbm, tab, local_sem.at[4]),
        pltpu.make_async_copy(curl_hbm.at[pl.ds(OWN * samp, OWN)], curl, local_sem.at[5]),
    ]
    barrier = pltpu.get_barrier_semaphore()

    @pl.when(is_hub)
    def _():
        def greet(group, other):
            pl.semaphore_signal(barrier, inc=1, device_id=at(group, other), device_id_type=MESH)

        for other in hubs:
            greet(space, other)
            greet(before, other)
        for other in reversed(plain):
            greet(space, other)
            greet(before, other)
        greet(before, home)
        for load in loads[4:]:
            load.start()

    for load in loads[:4]:
        load.start()

    loads[0].wait()
    loads[1].wait()
    pattern = pat[...].T
    rows = jnp.concatenate(
        [jnp.broadcast_to(pattern[e : e + 1, :], (2 * LINKS, LINKS)) for e in range(TILES)], axis=0
    )
    row = lax.broadcasted_iota(jnp.int32, (TILES * LINKS * 2, LINKS), 0)
    col = lax.broadcasted_iota(jnp.int32, (TILES * LINKS * 2, LINKS), 1)
    spot = jnp.sum(jnp.where(row // 2 % LINKS == col, rows, 0), axis=1, keepdims=True)
    row = lax.broadcasted_iota(jnp.int32, (TILES * LINKS * 2, TILES * 2), 0)
    col = lax.broadcasted_iota(jnp.int32, (TILES * LINKS * 2, TILES * 2), 1)
    hits = jnp.where((spot == col // 2 + 1) & (row % 2 == col % 2), 1.0, 0.0)
    own = coef[...].astype(F32)
    own = jnp.concatenate([own[:, w * TILE : (w + 1) * TILE] for w in range(TILES)], axis=0)
    picked = jnp.dot(hits.astype(BF16), own.astype(BF16), preferred_element_type=F32)
    picks[...] = picked.reshape(HUBS, OWN, EDGE, TILE).astype(BF16)
    spread = hits.T.astype(BF16)
    spread = jnp.concatenate([spread, spread], axis=1)

    loads[2].wait()
    loads[3].wait()
    links, laws = [], []
    for v in range(OWN):
        element = OWN * samp + v
        own_row = lax.broadcasted_iota(jnp.int32, (TILES, LINKS), 0) == element
        links.append(jnp.sum(jnp.where(own_row, pattern, 0), axis=0, keepdims=True))
        region = reg[...].reshape(1, TILES)
        lane = lax.broadcasted_iota(jnp.int32, (1, TILES), 1)
        region = jnp.sum(jnp.where(lane == element, region, 0), axis=1, keepdims=True)
        lane = lax.broadcasted_iota(jnp.int32, (3, 4), 1)
        own_law = jnp.sum(jnp.where(lane == region, law[...], 0.0), axis=1, keepdims=True)
        laws.append((own_law[0:1], own_law[1:2], own_law[2:3]))

    @pl.when(is_hub)
    def _():
        loads[4].wait()
        loads[5].wait()

    def remote(src, dst, i, group, other):
        return pltpu.make_async_remote_copy(
            src_ref=src, dst_ref=dst, send_sem=send_sem.at[i], recv_sem=recv_sem.at[i],
            device_id=at(group, other), device_id_type=MESH,
        )

    pl.semaphore_wait(barrier, jnp.where(is_hub, 2 * HUBS - 1, 2 * HUBS))

    @pl.when(is_hub)
    def _():
        pl.semaphore_signal(ready, inc=1, device_id=at(after, rank), device_id_type=MESH)

    first, last = coef.at[:, pl.ds(0, TILE)], coef.at[:, pl.ds((TILES - 1) * TILE, TILE)]
    sent_first = [remote(first, firsts.at[rank], 0, space, other) for other in hubs]
    sent_last = [remote(last, low_got.at[rank], 1, after, other) for other in [home, *hubs]]
    sent_picks = [remote(picks.at[other - HUB], got.at[rank], 3, space, other) for other in hubs]
    home_first = remote(first, firsts.at[rank], 0, space, home)
    home_picks = remote(picks.at[samp], got.at[rank], 3, space, home)

    @pl.when(jnp.logical_not(is_hub))
    def _():
        home_first.start()

    for copy in sent_first + sent_last:
        copy.start()

    @pl.when(jnp.logical_not(is_hub))
    def _():
        home_picks.start()

    for copy in sent_picks:
        copy.start()

    def block(ref, which):
        start = which * ROWS if isinstance(which, int) else pl.multiple_of(which * ROWS, ROWS)
        return ref.at[pl.ds(start, ROWS)]

    @pl.when(is_hub)
    def _():
        firsts[rank] = coef[:, 0:TILE]
        got[rank] = picks[samp]
        for v in range(OWN):
            curl_t[v] = curl[v].reshape(LINKS * TILE, COMP).T
        gathered = firsts.at[pl.ds(0, GROUP - 1)]
        remote(gathered, gathered, 0, space, hubs[0]).wait_recv()
        pl.semaphore_wait(ready, 1)
        handed = remote(firsts, high_got, 2, before, rank)
        handed.start()
        picked = got.at[pl.ds(0, GROUP - 1)]
        remote(picked, picked, 3, space, hubs[0]).wait_recv()
        windows = jnp.concatenate(
            [got[:, v].reshape(GROUP * EDGE, TILE) for v in range(OWN)], axis=1
        )
        waves = jnp.dot(
            tab[0:WAVES, :],
            jnp.concatenate([windows, windows], axis=0),
            preferred_element_type=F32,
        )
        remote(low_got, low_got, 1, space, hubs[0]).wait_recv()
        handed.wait_recv()
        halo = [
            ref[...].astype(F32).reshape(PARTS, TILE).astype(BF16) for ref in (low_got, high_got)
        ]
        halo = jnp.dot(
            tab[WAVES : WAVES + 2 * HALF, 0:TILE],
            jnp.concatenate([*halo, *halo], axis=0),
            preferred_element_type=F32,
        )
        halo = [halo[:HALF], halo[HALF:]]
        back = tab[WAVES + 2 * HALF : WAVES + 2 * HALF + PARTS, 0 : 3 * HALF]
        edges = [jnp.zeros((PARTS, TILE), F32), jnp.zeros((PARTS, TILE), F32)]
        densities = []
        for v in range(OWN):
            wave = []
            for k in range(LINKS):
                piece = waves[k * HALF : (k + 1) * HALF, v * TILE : (v + 1) * TILE]
                for i, spot in enumerate((0, TILES + 1)):
                    piece = piece + jnp.where(links[v][:, k : k + 1] == spot, halo[i], 0.0)
                wave.append(piece)
            densities.append(
                jnp.dot(
                    jnp.concatenate(split(jnp.concatenate(wave, axis=1)), axis=0),
                    curl[v].reshape(LINKS * TILE, COMP),
                    preferred_element_type=F32,
                )
            )
        fields = []
        for v in range(OWN):
            density = densities[v][:HALF] + densities[v][HALF:]
            comps = [density[:, c * TILE : (c + 1) * TILE] for c in range(3)]
            square = comps[0] * comps[0] + comps[1] * comps[1] + comps[2] * comps[2]
            base, knee, rise = laws[v]
            reluct = base + rise * square / (square + knee)
            high, low = split(jnp.concatenate([reluct * c for c in comps], axis=1))
            fields.append(jnp.concatenate([high, high, low], axis=0))
        harmonics = [jnp.dot(back, f, preferred_element_type=F32).astype(BF16) for f in fields]
        contribs = [
            jnp.dot(harmonics[v], curl_t[v], preferred_element_type=F32) for v in range(OWN)
        ]
        for v in range(OWN):
            for k in range(LINKS):
                tile = contribs[v][:, k * TILE : (k + 1) * TILE]
                for i, spot in enumerate((0, TILES + 1)):
                    edges[i] = edges[i] + jnp.where(links[v][:, k : k + 1] == spot, tile, 0.0)
        for i in range(2):
            for p in range(2):
                edge_flow[i, :, p, :] = edges[i][p * GROUP : (p + 1) * GROUP]

        to_after = [remote(edge_flow.at[1, o], low_flow.at[samp], 4, after, o) for o in launched]
        to_before = [remote(edge_flow.at[0, o], high_flow.at[samp], 5, before, o) for o in launched]
        to_group = [remote(block(flow, o), block(flow_got, samp), 6, space, o) for o in launched]
        for copy in to_after:
            copy.start()
        for v in range(OWN):
            for k in range(LINKS):
                for p in range(2):
                    flow[pl.ds(v * EDGE + 2 * k + p, GROUP, stride=ROWS), :] = contribs[v][
                        p * GROUP : (p + 1) * GROUP, k * TILE : (k + 1) * TILE
                    ]
        for other, *copies in zip(launched, to_group, to_before):

            @pl.when(rank != other)
            def _():
                copies[0].start()

            copies[1].start()
        mine = pl.ds(pl.multiple_of(samp * ROWS, ROWS), ROWS)
        flow_got[mine, :] = flow[pl.ds(pl.multiple_of(rank * ROWS, ROWS), ROWS), :]
        others = pl.ds(0, (HUBS - 1) * ROWS)
        remote(flow_got.at[others], flow_got.at[others], 6, space, hubs[0]).wait_recv()

    @pl.when(jnp.logical_not(is_hub))
    def _():
        remote(flow_got, flow_got, 6, space, home).wait_recv()

    remote(low_flow, low_flow, 4, after, home).wait_recv()
    remote(high_flow, high_flow, 5, after, home).wait_recv()
    owned = jnp.dot(
        spread, jnp.concatenate(split(flow_got[...]), axis=0), preferred_element_type=F32
    )
    low_sum, high_sum = low_flow[0], high_flow[0]
    for u in range(1, HUBS):
        low_sum, high_sum = low_sum + low_flow[u], high_sum + high_flow[u]
    for w in range(TILES):
        piece = owned[2 * w : 2 * w + 2]
        if w == 0:
            piece = piece + low_sum
        if w == TILES - 1:
            piece = piece + high_sum
        out_ref[:, w * TILE : (w + 1) * TILE] = piece
    for copy in sent_first + sent_last + sent_picks:
        copy.wait_send()

    @pl.when(jnp.logical_not(is_hub))
    def _():
        home_first.wait_send()
        home_picks.wait_send()

    @pl.when(is_hub)
    def _():
        others = pl.ds(0, (GROUP - 1) * ROWS)
        remote(firsts, high_got, 2, before, rank).wait_send()
        remote(edge_flow.at[1], edge_flow.at[1], 4, after, home).wait_send()
        remote(edge_flow.at[0], edge_flow.at[0], 5, after, home).wait_send()
        remote(flow.at[others], flow.at[others], 6, after, home).wait_send()


def per_device(coeffs, curl_tiles, pattern, region_ids, material_law, source):
    anywhere = pl.BlockSpec(memory_space=pltpu.HBM)
    table = tables()
    total = pl.pallas_call(
        kernel,
        out_shape=pltpu.VMEM(source.shape, F32),
        in_specs=[anywhere] * 6,
        out_specs=pl.BlockSpec(memory_space=pltpu.VMEM),
        scratch_shapes=[
            pltpu.VMEM((2, TILES * TILE), BF16),
            pltpu.VMEM((OWN, LINKS, TILE, COMP), BF16),
            pltpu.VMEM((LINKS, TILES), jnp.int32),
            pltpu.VMEM((TILES,), jnp.int32),
            pltpu.VMEM((3, 4), F32),
            pltpu.VMEM(table.shape, BF16),
            pltpu.VMEM((HUBS, OWN, EDGE, TILE), BF16),
            pltpu.VMEM((GROUP, OWN, EDGE, TILE), BF16),
            pltpu.VMEM((GROUP, 2, TILE), BF16),
            pltpu.VMEM((GROUP, 2, TILE), BF16),
            pltpu.VMEM((GROUP, 2, TILE), BF16),
            pltpu.VMEM((GROUP * ROWS, TILE), F32),
            pltpu.VMEM((HUBS * ROWS, TILE), F32),
            pltpu.VMEM((2, GROUP, 2, TILE), F32),
            pltpu.VMEM((HUBS, 2, TILE), F32),
            pltpu.VMEM((HUBS, 2, TILE), F32),
            pltpu.SemaphoreType.DMA((6,)),
            pltpu.SemaphoreType.DMA((7,)),
            pltpu.SemaphoreType.DMA((7,)),
            pltpu.SemaphoreType.REGULAR,
            pltpu.VMEM((OWN, COMP, LINKS * TILE), BF16),
        ],
        compiler_params=pltpu.CompilerParams(collective_id=0, has_side_effects=True),
        name="residual",
    )(coeffs, curl_tiles, pattern.T, region_ids, material_law, jnp.asarray(table))
    return total - source


def solution(mesh):
    placed = (
        P(("harm", "samp"), "space"),
        P("space", None, None, None),
        P("space", None),
        P("space"),
        P(),
        P(("harm", "samp"), "space"),
    )
    return jax.shard_map(
        per_device,
        mesh=mesh,
        in_specs=placed,
        out_specs=P(("harm", "samp"), "space"),
        check_vma=False,
    )
```

```python
import math

import jax
import jax.numpy as jnp
import ml_dtypes
import numpy as np
from jax import lax
from jax.experimental import pallas as pl
from jax.experimental.pallas import tpu as pltpu
from jax.sharding import PartitionSpec as P

SAMPLES = 64
HALF = SAMPLES // 2
PARTS = 32
GROUP = 16
HUBS = 4
OWN = 4
SPACE = 16
TILES = 16
LINKS = 4
TILE = 128
COMP = 3 * TILE
EDGE = LINKS * 2
ROWS = OWN * EDGE
WAVES = LINKS * HALF
MESH = pl.DeviceIdType.MESH
F32, BF16 = jnp.float32, jnp.bfloat16


def two_pieces(table):
    high = table.astype(ml_dtypes.bfloat16)
    low = (table - high.astype(np.float64)).astype(ml_dtypes.bfloat16)
    return high, low


def tables():
    t = np.arange(HALF)[:, None]
    q = np.arange(PARTS)[None, :]
    phase = ((2 * (q // 2) + 1) * t % SAMPLES) * (2.0 * math.pi / SAMPLES)
    transform = np.where(q % 2 == 0, np.cos(phase), np.sin(phase))
    by_rank = transform.reshape(HALF, GROUP, 2)
    main = np.zeros((LINKS, HALF, GROUP, LINKS, 2))
    for k in range(LINKS):
        main[k, :, :, k, :] = by_rank
    main = np.concatenate(two_pieces(main.reshape(WAVES, TILE)), axis=1)
    halo = np.zeros((2, HALF, 2, 2, PARTS), ml_dtypes.bfloat16)
    for piece, part in enumerate(two_pieces(transform)):
        for side in range(2):
            halo[side, :, piece, side] = part
    halo = np.pad(halo.reshape(2 * HALF, TILE), ((0, 0), (0, TILE)))
    back = (4.0 / SAMPLES) * by_rank.transpose(2, 1, 0).reshape(PARTS, HALF)
    back_high, back_low = two_pieces(back)
    back_row = np.zeros((PARTS, 2 * TILE), ml_dtypes.bfloat16)
    back_row[:, : 3 * HALF] = np.concatenate([back_high, back_low, back_high], axis=1)
    return np.concatenate([main, halo, back_row], axis=0)


def split(value):
    high = value.astype(BF16)
    return high, (value - high.astype(F32)).astype(BF16)


def kernel(
    coef_hbm, curl_hbm, pat_hbm, reg_hbm, law_hbm, tab_hbm, out_ref,
    coef, curl, pat, reg, law, tab, picks, got, firsts, low_got, high_got,
    flow, flow_got, edge_flow, low_flow, high_flow, local_sem, send_sem, recv_sem, ready, curl_t,
):
    harm, space, samp = lax.axis_index("harm"), lax.axis_index("space"), lax.axis_index("samp")
    rank = harm * 4 + samp
    is_hub = jnp.logical_or(jnp.logical_and(harm == 1, samp < 3), rank == 0)
    spoke = jnp.where(rank == 0, 3, samp)
    after, before = lax.rem(space + 1, SPACE), lax.rem(space + SPACE - 1, SPACE)

    def at(group, other):
        if isinstance(other, int):
            return (other // 4, group, other % 4)
        return (other // 4, group, lax.rem(other, 4))

    def hub_rank(u):
        return jnp.where(u == 3, 0, 4 + u)

    home = hub_rank(spoke)
    others_spokes = [lax.rem(spoke + d, HUBS) for d in range(1, HUBS)]
    hubs = [hub_rank(u) for u in others_spokes]
    launched = [(z // 4 * 2 + c) * 4 + z % 4 for z in range(8) for c in (1, 0)]
    plain = [other for other in launched if other not in (0, 4, 5, 6)]

    loads = [
        pltpu.make_async_copy(coef_hbm, coef, local_sem.at[0]),
        pltpu.make_async_copy(pat_hbm, pat, local_sem.at[1]),
        pltpu.make_async_copy(reg_hbm, reg, local_sem.at[2]),
        pltpu.make_async_copy(law_hbm, law, local_sem.at[3]),
        pltpu.make_async_copy(tab_hbm, tab, local_sem.at[4]),
        pltpu.make_async_copy(curl_hbm.at[pl.ds(OWN * spoke, OWN)], curl, local_sem.at[5]),
    ]
    barrier = pltpu.get_barrier_semaphore()

    @pl.when(is_hub)
    def _():
        def greet(group, other):
            pl.semaphore_signal(barrier, inc=1, device_id=at(group, other), device_id_type=MESH)

        for other in hubs:
            greet(space, other)
            greet(before, other)
        for other in reversed(plain):
            greet(space, other)
            greet(before, other)
        greet(before, home)
        for load in loads[4:]:
            load.start()

    for load in loads[:4]:
        load.start()

    loads[0].wait()
    loads[1].wait()
    pattern = pat[...].T
    rows = jnp.concatenate(
        [jnp.broadcast_to(pattern[e : e + 1, :], (2 * LINKS, LINKS)) for e in range(TILES)], axis=0
    )
    row = lax.broadcasted_iota(jnp.int32, (TILES * LINKS * 2, LINKS), 0)
    col = lax.broadcasted_iota(jnp.int32, (TILES * LINKS * 2, LINKS), 1)
    spot = jnp.sum(jnp.where(row // 2 % LINKS == col, rows, 0), axis=1, keepdims=True)
    row = lax.broadcasted_iota(jnp.int32, (TILES * LINKS * 2, TILES * 2), 0)
    col = lax.broadcasted_iota(jnp.int32, (TILES * LINKS * 2, TILES * 2), 1)
    hits = jnp.where((spot == col // 2 + 1) & (row % 2 == col % 2), 1.0, 0.0)
    own = coef[...].astype(F32)
    own = jnp.concatenate([own[:, w * TILE : (w + 1) * TILE] for w in range(TILES)], axis=0)
    picked = jnp.dot(hits.astype(BF16), own.astype(BF16), preferred_element_type=F32)
    picks[...] = picked.reshape(HUBS, OWN, EDGE, TILE).astype(BF16)
    spread = hits.T.astype(BF16)
    spread = jnp.concatenate([spread, spread], axis=1)

    loads[2].wait()
    loads[3].wait()
    links, laws = [], []
    for v in range(OWN):
        element = OWN * spoke + v
        own_row = lax.broadcasted_iota(jnp.int32, (TILES, LINKS), 0) == element
        links.append(jnp.sum(jnp.where(own_row, pattern, 0), axis=0, keepdims=True))
        region = reg[...].reshape(1, TILES)
        lane = lax.broadcasted_iota(jnp.int32, (1, TILES), 1)
        region = jnp.sum(jnp.where(lane == element, region, 0), axis=1, keepdims=True)
        lane = lax.broadcasted_iota(jnp.int32, (3, 4), 1)
        own_law = jnp.sum(jnp.where(lane == region, law[...], 0.0), axis=1, keepdims=True)
        laws.append((own_law[0:1], own_law[1:2], own_law[2:3]))

    @pl.when(is_hub)
    def _():
        loads[4].wait()
        loads[5].wait()

    def remote(src, dst, i, group, other):
        return pltpu.make_async_remote_copy(
            src_ref=src, dst_ref=dst, send_sem=send_sem.at[i], recv_sem=recv_sem.at[i],
            device_id=at(group, other), device_id_type=MESH,
        )

    pl.semaphore_wait(barrier, jnp.where(is_hub, 2 * HUBS - 1, 2 * HUBS))

    @pl.when(is_hub)
    def _():
        pl.semaphore_signal(ready, inc=1, device_id=at(after, rank), device_id_type=MESH)

    first, last = coef.at[:, pl.ds(0, TILE)], coef.at[:, pl.ds((TILES - 1) * TILE, TILE)]
    sent_first = [remote(first, firsts.at[rank], 0, space, other) for other in hubs]
    sent_last = [remote(last, low_got.at[rank], 1, after, other) for other in [home, *hubs]]
    sent_picks = [
        remote(picks.at[u], got.at[rank], 3, space, hub_rank(u)) for u in others_spokes
    ]
    home_first = remote(first, firsts.at[rank], 0, space, home)
    home_picks = remote(picks.at[spoke], got.at[rank], 3, space, home)

    @pl.when(jnp.logical_not(is_hub))
    def _():
        home_first.start()

    for copy in sent_first + sent_last:
        copy.start()

    @pl.when(jnp.logical_not(is_hub))
    def _():
        home_picks.start()

    for copy in sent_picks:
        copy.start()

    def block(ref, which):
        start = which * ROWS if isinstance(which, int) else pl.multiple_of(which * ROWS, ROWS)
        return ref.at[pl.ds(start, ROWS)]

    @pl.when(is_hub)
    def _():
        firsts[rank] = coef[:, 0:TILE]
        got[rank] = picks[spoke]
        for v in range(OWN):
            curl_t[v] = curl[v].reshape(LINKS * TILE, COMP).T
        gathered = firsts.at[pl.ds(0, GROUP - 1)]
        remote(gathered, gathered, 0, space, hubs[0]).wait_recv()
        pl.semaphore_wait(ready, 1)
        handed = remote(firsts, high_got, 2, before, rank)
        handed.start()
        picked = got.at[pl.ds(0, GROUP - 1)]
        remote(picked, picked, 3, space, hubs[0]).wait_recv()
        windows = jnp.concatenate(
            [got[:, v].reshape(GROUP * EDGE, TILE) for v in range(OWN)], axis=1
        )
        waves = jnp.dot(
            tab[0:WAVES, :],
            jnp.concatenate([windows, windows], axis=0),
            preferred_element_type=F32,
        )
        remote(low_got, low_got, 1, space, hubs[0]).wait_recv()
        handed.wait_recv()
        halo = [
            ref[...].astype(F32).reshape(PARTS, TILE).astype(BF16) for ref in (low_got, high_got)
        ]
        halo = jnp.dot(
            tab[WAVES : WAVES + 2 * HALF, 0:TILE],
            jnp.concatenate([*halo, *halo], axis=0),
            preferred_element_type=F32,
        )
        halo = [halo[:HALF], halo[HALF:]]
        back = tab[WAVES + 2 * HALF : WAVES + 2 * HALF + PARTS, 0 : 3 * HALF]
        edges = [jnp.zeros((PARTS, TILE), F32), jnp.zeros((PARTS, TILE), F32)]
        densities = []
        for v in range(OWN):
            wave = []
            for k in range(LINKS):
                piece = waves[k * HALF : (k + 1) * HALF, v * TILE : (v + 1) * TILE]
                for i, spot in enumerate((0, TILES + 1)):
                    piece = piece + jnp.where(links[v][:, k : k + 1] == spot, halo[i], 0.0)
                wave.append(piece)
            densities.append(
                jnp.dot(
                    jnp.concatenate(split(jnp.concatenate(wave, axis=1)), axis=0),
                    curl[v].reshape(LINKS * TILE, COMP),
                    preferred_element_type=F32,
                )
            )
        fields = []
        for v in range(OWN):
            density = densities[v][:HALF] + densities[v][HALF:]
            comps = [density[:, c * TILE : (c + 1) * TILE] for c in range(3)]
            square = comps[0] * comps[0] + comps[1] * comps[1] + comps[2] * comps[2]
            base, knee, rise = laws[v]
            reluct = base + rise * square / (square + knee)
            high, low = split(jnp.concatenate([reluct * c for c in comps], axis=1))
            fields.append(jnp.concatenate([high, high, low], axis=0))
        harmonics = [jnp.dot(back, f, preferred_element_type=F32).astype(BF16) for f in fields]
        contribs = [
            jnp.dot(harmonics[v], curl_t[v], preferred_element_type=F32) for v in range(OWN)
        ]
        for v in range(OWN):
            for k in range(LINKS):
                tile = contribs[v][:, k * TILE : (k + 1) * TILE]
                for i, spot in enumerate((0, TILES + 1)):
                    edges[i] = edges[i] + jnp.where(links[v][:, k : k + 1] == spot, tile, 0.0)
        for i in range(2):
            for p in range(2):
                edge_flow[i, :, p, :] = edges[i][p * GROUP : (p + 1) * GROUP]

        to_after = [remote(edge_flow.at[1, o], low_flow.at[spoke], 4, after, o) for o in launched]
        to_before = [remote(edge_flow.at[0, o], high_flow.at[spoke], 5, before, o) for o in launched]
        to_group = [remote(block(flow, o), block(flow_got, spoke), 6, space, o) for o in launched]
        for copy in to_after:
            copy.start()
        for v in range(OWN):
            for k in range(LINKS):
                for p in range(2):
                    flow[pl.ds(v * EDGE + 2 * k + p, GROUP, stride=ROWS), :] = contribs[v][
                        p * GROUP : (p + 1) * GROUP, k * TILE : (k + 1) * TILE
                    ]
        for other, *copies in zip(launched, to_group, to_before):

            @pl.when(rank != other)
            def _():
                copies[0].start()

            copies[1].start()
        mine = pl.ds(pl.multiple_of(spoke * ROWS, ROWS), ROWS)
        flow_got[mine, :] = flow[pl.ds(pl.multiple_of(rank * ROWS, ROWS), ROWS), :]
        others = pl.ds(0, (HUBS - 1) * ROWS)
        remote(flow_got.at[others], flow_got.at[others], 6, space, hubs[0]).wait_recv()

    @pl.when(jnp.logical_not(is_hub))
    def _():
        remote(flow_got, flow_got, 6, space, home).wait_recv()

    owned = jnp.dot(
        spread, jnp.concatenate(split(flow_got[...]), axis=0), preferred_element_type=F32
    )
    for w in range(1, TILES - 1):
        out_ref[:, w * TILE : (w + 1) * TILE] = owned[2 * w : 2 * w + 2]
    for copy in sent_first + sent_last + sent_picks:
        copy.wait_send()

    @pl.when(jnp.logical_not(is_hub))
    def _():
        home_first.wait_send()
        home_picks.wait_send()

    @pl.when(is_hub)
    def _():
        others = pl.ds(0, (GROUP - 1) * ROWS)
        remote(firsts, high_got, 2, before, rank).wait_send()
        remote(edge_flow.at[1], edge_flow.at[1], 4, after, home).wait_send()
        remote(edge_flow.at[0], edge_flow.at[0], 5, after, home).wait_send()
        remote(flow.at[others], flow.at[others], 6, after, home).wait_send()

    for w, edge, i in ((TILES - 1, high_flow, 5), (0, low_flow, 4)):
        remote(edge, edge, i, after, home).wait_recv()
        edge_sum = (edge[0] + edge[1]) + (edge[2] + edge[3])
        out_ref[:, w * TILE : (w + 1) * TILE] = owned[2 * w : 2 * w + 2] + edge_sum


def per_device(coeffs, curl_tiles, pattern, region_ids, material_law, source):
    anywhere = pl.BlockSpec(memory_space=pltpu.HBM)
    table = tables()
    total = pl.pallas_call(
        kernel,
        out_shape=pltpu.VMEM(source.shape, F32),
        in_specs=[anywhere] * 6,
        out_specs=pl.BlockSpec(memory_space=pltpu.VMEM),
        scratch_shapes=[
            pltpu.VMEM((2, TILES * TILE), BF16),
            pltpu.VMEM((OWN, LINKS, TILE, COMP), BF16),
            pltpu.VMEM((LINKS, TILES), jnp.int32),
            pltpu.VMEM((TILES,), jnp.int32),
            pltpu.VMEM((3, 4), F32),
            pltpu.VMEM(table.shape, BF16),
            pltpu.VMEM((HUBS, OWN, EDGE, TILE), BF16),
            pltpu.VMEM((GROUP, OWN, EDGE, TILE), BF16),
            pltpu.VMEM((GROUP, 2, TILE), BF16),
            pltpu.VMEM((GROUP, 2, TILE), BF16),
            pltpu.VMEM((GROUP, 2, TILE), BF16),
            pltpu.VMEM((GROUP * ROWS, TILE), F32),
            pltpu.VMEM((HUBS * ROWS, TILE), F32),
            pltpu.VMEM((2, GROUP, 2, TILE), F32),
            pltpu.VMEM((HUBS, 2, TILE), F32),
            pltpu.VMEM((HUBS, 2, TILE), F32),
            pltpu.SemaphoreType.DMA((6,)),
            pltpu.SemaphoreType.DMA((7,)),
            pltpu.SemaphoreType.DMA((7,)),
            pltpu.SemaphoreType.REGULAR,
            pltpu.VMEM((OWN, COMP, LINKS * TILE), BF16),
        ],
        compiler_params=pltpu.CompilerParams(collective_id=0, has_side_effects=True),
        name="residual",
    )(coeffs, curl_tiles, pattern.T, region_ids, material_law, jnp.asarray(table))
    return total - source


def solution(mesh):
    placed = (
        P(("harm", "samp"), "space"),
        P("space", None, None, None),
        P("space", None),
        P("space"),
        P(),
        P(("harm", "samp"), "space"),
    )
    return jax.shard_map(
        per_device,
        mesh=mesh,
        in_specs=placed,
        out_specs=P(("harm", "samp"), "space"),
        check_vma=False,
    )
```

```python
import math

import jax
import jax.numpy as jnp
import ml_dtypes
import numpy as np
from jax import lax
from jax.experimental import pallas as pl
from jax.experimental.pallas import tpu as pltpu
from jax.sharding import PartitionSpec as P

SAMPLES = 64
HALF = SAMPLES // 2
PARTS = 32
GROUP = 16
HUBS = 4
OWN = 4
SPACE = 16
TILES = 16
LINKS = 4
TILE = 128
COMP = 3 * TILE
EDGE = LINKS * 2
ROWS = OWN * EDGE
WAVES = LINKS * HALF
MESH = pl.DeviceIdType.MESH
F32, BF16 = jnp.float32, jnp.bfloat16


def two_pieces(table):
    high = table.astype(ml_dtypes.bfloat16)
    low = (table - high.astype(np.float64)).astype(ml_dtypes.bfloat16)
    return high, low


def tables():
    t = np.arange(HALF)[:, None]
    q = np.arange(PARTS)[None, :]
    phase = ((2 * (q // 2) + 1) * t % SAMPLES) * (2.0 * math.pi / SAMPLES)
    transform = np.where(q % 2 == 0, np.cos(phase), np.sin(phase))
    by_rank = transform.reshape(HALF, GROUP, 2)
    main = np.zeros((LINKS, HALF, GROUP, LINKS, 2))
    for k in range(LINKS):
        main[k, :, :, k, :] = by_rank
    main = np.concatenate(two_pieces(main.reshape(WAVES, TILE)), axis=1)
    halo = np.zeros((2, HALF, 2, 2, PARTS), ml_dtypes.bfloat16)
    for piece, part in enumerate(two_pieces(transform)):
        for side in range(2):
            halo[side, :, piece, side] = part
    halo = np.pad(halo.reshape(2 * HALF, TILE), ((0, 0), (0, TILE)))
    back = (4.0 / SAMPLES) * by_rank.transpose(2, 1, 0).reshape(PARTS, HALF)
    back_high, back_low = two_pieces(back)
    back_row = np.zeros((PARTS, 2 * TILE), ml_dtypes.bfloat16)
    back_row[:, : 3 * HALF] = np.concatenate([back_high, back_low, back_high], axis=1)
    return np.concatenate([main, halo, back_row], axis=0)


def split(value):
    high = value.astype(BF16)
    return high, (value - high.astype(F32)).astype(BF16)


def kernel(
    coef_hbm, curl_hbm, pat_hbm, reg_hbm, law_hbm, tab_hbm, out_ref,
    coef, curl, pat, reg, law, tab, picks, got, firsts, low_got, high_got,
    flow, flow_got, edge_flow, low_flow, high_flow, local_sem, send_sem, recv_sem, ready, curl_t,
):
    harm, space, samp = lax.axis_index("harm"), lax.axis_index("space"), lax.axis_index("samp")
    rank = harm * 4 + samp
    is_hub = jnp.logical_or(jnp.logical_and(harm == 1, samp < 3), rank == 0)
    spoke = jnp.where(rank == 0, 3, samp)
    after, before = lax.rem(space + 1, SPACE), lax.rem(space + SPACE - 1, SPACE)

    def at(group, other):
        if isinstance(other, int):
            return (other // 4, group, other % 4)
        return (other // 4, group, lax.rem(other, 4))

    def hub_rank(u):
        return jnp.where(u == 3, 0, 4 + u)

    home = hub_rank(spoke)
    others_spokes = [lax.rem(spoke + d, HUBS) for d in range(1, HUBS)]
    hubs = [hub_rank(u) for u in others_spokes]
    launched = [(z // 4 * 2 + c) * 4 + z % 4 for z in range(8) for c in (1, 0)]
    plain = [other for other in launched if other not in (0, 4, 5, 6)]

    loads = [
        pltpu.make_async_copy(coef_hbm, coef, local_sem.at[0]),
        pltpu.make_async_copy(pat_hbm, pat, local_sem.at[1]),
        pltpu.make_async_copy(reg_hbm, reg, local_sem.at[2]),
        pltpu.make_async_copy(law_hbm, law, local_sem.at[3]),
        pltpu.make_async_copy(tab_hbm, tab, local_sem.at[4]),
        pltpu.make_async_copy(curl_hbm.at[pl.ds(OWN * spoke, OWN)], curl, local_sem.at[5]),
    ]
    barrier = pltpu.get_barrier_semaphore()

    @pl.when(is_hub)
    def _():
        def greet(group, other):
            pl.semaphore_signal(barrier, inc=1, device_id=at(group, other), device_id_type=MESH)

        for other in hubs:
            greet(space, other)
            greet(before, other)
        greet(before, home)
        for other in reversed(plain):
            greet(space, other)
            greet(before, other)
        for load in loads[4:]:
            load.start()

    for load in loads[:4]:
        load.start()

    loads[0].wait()
    loads[1].wait()
    pattern = pat[...].T
    rows = jnp.concatenate(
        [jnp.broadcast_to(pattern[e : e + 1, :], (2 * LINKS, LINKS)) for e in range(TILES)], axis=0
    )
    row = lax.broadcasted_iota(jnp.int32, (TILES * LINKS * 2, LINKS), 0)
    col = lax.broadcasted_iota(jnp.int32, (TILES * LINKS * 2, LINKS), 1)
    spot = jnp.sum(jnp.where(row // 2 % LINKS == col, rows, 0), axis=1, keepdims=True)
    row = lax.broadcasted_iota(jnp.int32, (TILES * LINKS * 2, TILES * 2), 0)
    col = lax.broadcasted_iota(jnp.int32, (TILES * LINKS * 2, TILES * 2), 1)
    hits = jnp.where((spot == col // 2 + 1) & (row % 2 == col % 2), 1.0, 0.0)
    own = coef[...].astype(F32)
    own = jnp.concatenate([own[:, w * TILE : (w + 1) * TILE] for w in range(TILES)], axis=0)
    picked = jnp.dot(hits.astype(BF16), own.astype(BF16), preferred_element_type=F32)
    picks[...] = picked.reshape(HUBS, OWN, EDGE, TILE).astype(BF16)
    spread = hits.T.astype(BF16)
    spread = jnp.concatenate([spread, spread], axis=1)

    loads[2].wait()
    loads[3].wait()
    links, laws = [], []
    for v in range(OWN):
        element = OWN * spoke + v
        own_row = lax.broadcasted_iota(jnp.int32, (TILES, LINKS), 0) == element
        links.append(jnp.sum(jnp.where(own_row, pattern, 0), axis=0, keepdims=True))
        region = reg[...].reshape(1, TILES)
        lane = lax.broadcasted_iota(jnp.int32, (1, TILES), 1)
        region = jnp.sum(jnp.where(lane == element, region, 0), axis=1, keepdims=True)
        lane = lax.broadcasted_iota(jnp.int32, (3, 4), 1)
        own_law = jnp.sum(jnp.where(lane == region, law[...], 0.0), axis=1, keepdims=True)
        laws.append((own_law[0:1], own_law[1:2], own_law[2:3]))

    @pl.when(is_hub)
    def _():
        loads[4].wait()
        loads[5].wait()

    def remote(src, dst, i, group, other):
        return pltpu.make_async_remote_copy(
            src_ref=src, dst_ref=dst, send_sem=send_sem.at[i], recv_sem=recv_sem.at[i],
            device_id=at(group, other), device_id_type=MESH,
        )

    pl.semaphore_wait(barrier, jnp.where(is_hub, 2 * HUBS - 1, 2 * HUBS))

    @pl.when(is_hub)
    def _():
        pl.semaphore_signal(ready, inc=1, device_id=at(after, rank), device_id_type=MESH)

    first, last = coef.at[:, pl.ds(0, TILE)], coef.at[:, pl.ds((TILES - 1) * TILE, TILE)]
    sent_first = [remote(first, firsts.at[rank], 0, space, other) for other in hubs]
    sent_last = [remote(last, low_got.at[rank], 1, after, other) for other in [home, *hubs]]
    sent_picks = [
        remote(picks.at[u], got.at[rank], 3, space, hub_rank(u)) for u in others_spokes
    ]
    home_first = remote(first, firsts.at[rank], 0, space, home)
    home_picks = remote(picks.at[spoke], got.at[rank], 3, space, home)

    @pl.when(jnp.logical_not(is_hub))
    def _():
        home_first.start()

    for copy in sent_first + sent_last:
        copy.start()

    @pl.when(jnp.logical_not(is_hub))
    def _():
        home_picks.start()

    for copy in sent_picks:
        copy.start()

    def block(ref, which):
        start = which * ROWS if isinstance(which, int) else pl.multiple_of(which * ROWS, ROWS)
        return ref.at[pl.ds(start, ROWS)]

    @pl.when(is_hub)
    def _():
        firsts[rank] = coef[:, 0:TILE]
        got[rank] = picks[spoke]
        for v in range(OWN):
            curl_t[v] = curl[v].reshape(LINKS * TILE, COMP).T
        gathered = firsts.at[pl.ds(0, GROUP - 1)]
        remote(gathered, gathered, 0, space, hubs[0]).wait_recv()
        pl.semaphore_wait(ready, 1)
        handed = remote(firsts, high_got, 2, before, rank)
        handed.start()
        picked = got.at[pl.ds(0, GROUP - 1)]
        remote(picked, picked, 3, space, hubs[0]).wait_recv()
        windows = jnp.concatenate(
            [got[:, v].reshape(GROUP * EDGE, TILE) for v in range(OWN)], axis=1
        )
        waves = jnp.dot(
            tab[0:WAVES, :],
            jnp.concatenate([windows, windows], axis=0),
            preferred_element_type=F32,
        )
        remote(low_got, low_got, 1, space, hubs[0]).wait_recv()
        handed.wait_recv()
        halo = [
            ref[...].astype(F32).reshape(PARTS, TILE).astype(BF16) for ref in (low_got, high_got)
        ]
        halo = jnp.dot(
            tab[WAVES : WAVES + 2 * HALF, 0:TILE],
            jnp.concatenate([*halo, *halo], axis=0),
            preferred_element_type=F32,
        )
        halo = [halo[:HALF], halo[HALF:]]
        back = tab[WAVES + 2 * HALF : WAVES + 2 * HALF + PARTS, 0 : 3 * HALF]
        edges = [jnp.zeros((PARTS, TILE), F32), jnp.zeros((PARTS, TILE), F32)]
        densities = []
        for v in range(OWN):
            wave = []
            for k in range(LINKS):
                piece = waves[k * HALF : (k + 1) * HALF, v * TILE : (v + 1) * TILE]
                for i, spot in enumerate((0, TILES + 1)):
                    piece = piece + jnp.where(links[v][:, k : k + 1] == spot, halo[i], 0.0)
                wave.append(piece)
            densities.append(
                jnp.dot(
                    jnp.concatenate(split(jnp.concatenate(wave, axis=1)), axis=0),
                    curl[v].reshape(LINKS * TILE, COMP),
                    preferred_element_type=F32,
                )
            )
        fields = []
        for v in range(OWN):
            density = densities[v][:HALF] + densities[v][HALF:]
            comps = [density[:, c * TILE : (c + 1) * TILE] for c in range(3)]
            square = comps[0] * comps[0] + comps[1] * comps[1] + comps[2] * comps[2]
            base, knee, rise = laws[v]
            reluct = base + rise * square / (square + knee)
            high, low = split(jnp.concatenate([reluct * c for c in comps], axis=1))
            fields.append(jnp.concatenate([high, high, low], axis=0))
        harmonics = [jnp.dot(back, f, preferred_element_type=F32).astype(BF16) for f in fields]
        contribs = [
            jnp.dot(harmonics[v], curl_t[v], preferred_element_type=F32) for v in range(OWN)
        ]
        for v in range(OWN):
            for k in range(LINKS):
                tile = contribs[v][:, k * TILE : (k + 1) * TILE]
                for i, spot in enumerate((0, TILES + 1)):
                    edges[i] = edges[i] + jnp.where(links[v][:, k : k + 1] == spot, tile, 0.0)
        for i in range(2):
            for p in range(2):
                edge_flow[i, :, p, :] = edges[i][p * GROUP : (p + 1) * GROUP]

        to_after = [remote(edge_flow.at[1, o], low_flow.at[spoke], 4, after, o) for o in launched]
        to_before = [remote(edge_flow.at[0, o], high_flow.at[spoke], 5, before, o) for o in launched]
        to_group = [remote(block(flow, o), block(flow_got, spoke), 6, space, o) for o in launched]
        for copy in to_after:
            copy.start()
        for v in range(OWN):
            for k in range(LINKS):
                for p in range(2):
                    flow[pl.ds(v * EDGE + 2 * k + p, GROUP, stride=ROWS), :] = contribs[v][
                        p * GROUP : (p + 1) * GROUP, k * TILE : (k + 1) * TILE
                    ]
        for other, *copies in zip(launched, to_group, to_before):

            @pl.when(rank != other)
            def _():
                copies[0].start()

            copies[1].start()
        mine = pl.ds(pl.multiple_of(spoke * ROWS, ROWS), ROWS)
        flow_got[mine, :] = flow[pl.ds(pl.multiple_of(rank * ROWS, ROWS), ROWS), :]
        others = pl.ds(0, (HUBS - 1) * ROWS)
        remote(flow_got.at[others], flow_got.at[others], 6, space, hubs[0]).wait_recv()

    @pl.when(jnp.logical_not(is_hub))
    def _():
        remote(flow_got, flow_got, 6, space, home).wait_recv()

    owned = jnp.dot(
        spread, jnp.concatenate(split(flow_got[...]), axis=0), preferred_element_type=F32
    )
    for w in range(1, TILES - 1):
        out_ref[:, w * TILE : (w + 1) * TILE] = owned[2 * w : 2 * w + 2]
    for copy in sent_first + sent_last + sent_picks:
        copy.wait_send()

    @pl.when(jnp.logical_not(is_hub))
    def _():
        home_first.wait_send()
        home_picks.wait_send()

    @pl.when(is_hub)
    def _():
        others = pl.ds(0, (GROUP - 1) * ROWS)
        remote(firsts, high_got, 2, before, rank).wait_send()
        remote(edge_flow.at[1], edge_flow.at[1], 4, after, home).wait_send()
        remote(edge_flow.at[0], edge_flow.at[0], 5, after, home).wait_send()
        remote(flow.at[others], flow.at[others], 6, after, home).wait_send()

    for w, edge, i in ((TILES - 1, high_flow, 5), (0, low_flow, 4)):
        remote(edge, edge, i, after, home).wait_recv()
        edge_sum = (edge[0] + edge[1]) + (edge[2] + edge[3])
        out_ref[:, w * TILE : (w + 1) * TILE] = owned[2 * w : 2 * w + 2] + edge_sum


def per_device(coeffs, curl_tiles, pattern, region_ids, material_law, source):
    anywhere = pl.BlockSpec(memory_space=pltpu.HBM)
    table = tables()
    total = pl.pallas_call(
        kernel,
        out_shape=pltpu.VMEM(source.shape, F32),
        in_specs=[anywhere] * 6,
        out_specs=pl.BlockSpec(memory_space=pltpu.VMEM),
        scratch_shapes=[
            pltpu.VMEM((2, TILES * TILE), BF16),
            pltpu.VMEM((OWN, LINKS, TILE, COMP), BF16),
            pltpu.VMEM((LINKS, TILES), jnp.int32),
            pltpu.VMEM((TILES,), jnp.int32),
            pltpu.VMEM((3, 4), F32),
            pltpu.VMEM(table.shape, BF16),
            pltpu.VMEM((HUBS, OWN, EDGE, TILE), BF16),
            pltpu.VMEM((GROUP, OWN, EDGE, TILE), BF16),
            pltpu.VMEM((GROUP, 2, TILE), BF16),
            pltpu.VMEM((GROUP, 2, TILE), BF16),
            pltpu.VMEM((GROUP, 2, TILE), BF16),
            pltpu.VMEM((GROUP * ROWS, TILE), F32),
            pltpu.VMEM((HUBS * ROWS, TILE), F32),
            pltpu.VMEM((2, GROUP, 2, TILE), F32),
            pltpu.VMEM((HUBS, 2, TILE), F32),
            pltpu.VMEM((HUBS, 2, TILE), F32),
            pltpu.SemaphoreType.DMA((6,)),
            pltpu.SemaphoreType.DMA((7,)),
            pltpu.SemaphoreType.DMA((7,)),
            pltpu.SemaphoreType.REGULAR,
            pltpu.VMEM((OWN, COMP, LINKS * TILE), BF16),
        ],
        compiler_params=pltpu.CompilerParams(collective_id=0, has_side_effects=True),
        name="residual",
    )(coeffs, curl_tiles, pattern.T, region_ids, material_law, jnp.asarray(table))
    return total - source


def solution(mesh):
    placed = (
        P(("harm", "samp"), "space"),
        P("space", None, None, None),
        P("space", None),
        P("space"),
        P(),
        P(("harm", "samp"), "space"),
    )
    return jax.shard_map(
        per_device,
        mesh=mesh,
        in_specs=placed,
        out_specs=P(("harm", "samp"), "space"),
        check_vma=False,
    )
```

```python
import math

import jax
import jax.numpy as jnp
import ml_dtypes
import numpy as np
from jax import lax
from jax.experimental import pallas as pl
from jax.experimental.pallas import tpu as pltpu
from jax.sharding import PartitionSpec as P

SAMPLES = 64
HALF = SAMPLES // 2
PARTS = 32
GROUP = 16
HUBS = 4
OWN = 4
SPACE = 16
TILES = 16
LINKS = 4
TILE = 128
COMP = 3 * TILE
EDGE = LINKS * 2
ROWS = OWN * EDGE
WAVES = LINKS * HALF
MESH = pl.DeviceIdType.MESH
F32, BF16 = jnp.float32, jnp.bfloat16


def two_pieces(table):
    high = table.astype(ml_dtypes.bfloat16)
    low = (table - high.astype(np.float64)).astype(ml_dtypes.bfloat16)
    return high, low


def tables():
    t = np.arange(HALF)[:, None]
    q = np.arange(PARTS)[None, :]
    phase = ((2 * (q // 2) + 1) * t % SAMPLES) * (2.0 * math.pi / SAMPLES)
    transform = np.where(q % 2 == 0, np.cos(phase), np.sin(phase))
    by_rank = transform.reshape(HALF, GROUP, 2)
    main = np.zeros((LINKS, HALF, GROUP, LINKS, 2))
    for k in range(LINKS):
        main[k, :, :, k, :] = by_rank
    main = np.concatenate(two_pieces(main.reshape(WAVES, TILE)), axis=1)
    halo = np.zeros((2, HALF, 2, 2, PARTS), ml_dtypes.bfloat16)
    for piece, part in enumerate(two_pieces(transform)):
        for side in range(2):
            halo[side, :, piece, side] = part
    halo = np.pad(halo.reshape(2 * HALF, TILE), ((0, 0), (0, TILE)))
    back = (4.0 / SAMPLES) * by_rank.transpose(2, 1, 0).reshape(PARTS, HALF)
    back_high, back_low = two_pieces(back)
    back_row = np.zeros((PARTS, 2 * TILE), ml_dtypes.bfloat16)
    back_row[:, : 3 * HALF] = np.concatenate([back_high, back_low, back_high], axis=1)
    return np.concatenate([main, halo, back_row], axis=0)


def split(value):
    high = value.astype(BF16)
    return high, (value - high.astype(F32)).astype(BF16)


def kernel(
    coef_hbm, curl_hbm, pat_hbm, reg_hbm, law_hbm, tab_hbm, out_ref,
    coef, curl, pat, reg, law, tab, picks, got, firsts, low_got, high_got,
    flow, flow_got, edge_flow, low_flow, high_flow, local_sem, send_sem, recv_sem, ready, curl_t,
):
    harm, space, samp = lax.axis_index("harm"), lax.axis_index("space"), lax.axis_index("samp")
    rank = harm * 4 + samp
    is_hub = jnp.logical_or(jnp.logical_and(harm == 1, samp < 3), rank == 0)
    spoke = jnp.where(rank == 0, 3, samp)
    after, before = lax.rem(space + 1, SPACE), lax.rem(space + SPACE - 1, SPACE)

    def at(group, other):
        if isinstance(other, int):
            return (other // 4, group, other % 4)
        return (other // 4, group, lax.rem(other, 4))

    def hub_rank(u):
        return jnp.where(u == 3, 0, 4 + u)

    home = hub_rank(spoke)
    others_spokes = [lax.rem(spoke + d, HUBS) for d in range(1, HUBS)]
    hubs = [hub_rank(u) for u in others_spokes]
    launched = [(z // 4 * 2 + c) * 4 + z % 4 for z in range(8) for c in (1, 0)]
    plain = [other for other in launched if other not in (0, 4, 5, 6)]

    loads = [
        pltpu.make_async_copy(coef_hbm, coef, local_sem.at[0]),
        pltpu.make_async_copy(pat_hbm, pat, local_sem.at[1]),
        pltpu.make_async_copy(reg_hbm, reg, local_sem.at[2]),
        pltpu.make_async_copy(law_hbm, law, local_sem.at[3]),
        pltpu.make_async_copy(tab_hbm, tab, local_sem.at[4]),
        pltpu.make_async_copy(curl_hbm.at[pl.ds(OWN * spoke, OWN)], curl, local_sem.at[5]),
    ]
    barrier = pltpu.get_barrier_semaphore()

    @pl.when(is_hub)
    def _():
        def greet(group, other):
            pl.semaphore_signal(barrier, inc=1, device_id=at(group, other), device_id_type=MESH)

        for other in hubs:
            greet(space, other)
            greet(before, other)
        for other in reversed(plain):
            greet(space, other)
            greet(before, other)
        greet(before, home)
        for load in loads[4:]:
            load.start()

    for load in loads[:4]:
        load.start()

    loads[0].wait()
    loads[1].wait()
    pattern = pat[...].T
    rows = jnp.concatenate(
        [jnp.broadcast_to(pattern[e : e + 1, :], (2 * LINKS, LINKS)) for e in range(TILES)], axis=0
    )
    row = lax.broadcasted_iota(jnp.int32, (TILES * LINKS * 2, LINKS), 0)
    col = lax.broadcasted_iota(jnp.int32, (TILES * LINKS * 2, LINKS), 1)
    spot = jnp.sum(jnp.where(row // 2 % LINKS == col, rows, 0), axis=1, keepdims=True)
    row = lax.broadcasted_iota(jnp.int32, (TILES * LINKS * 2, TILES * 2), 0)
    col = lax.broadcasted_iota(jnp.int32, (TILES * LINKS * 2, TILES * 2), 1)
    hits = jnp.where((spot == col // 2 + 1) & (row % 2 == col % 2), 1.0, 0.0)
    own = coef[...].astype(F32)
    own = jnp.concatenate([own[:, w * TILE : (w + 1) * TILE] for w in range(TILES)], axis=0)
    picked = jnp.dot(hits.astype(BF16), own.astype(BF16), preferred_element_type=F32)
    picks[...] = picked.reshape(HUBS, OWN, EDGE, TILE).astype(BF16)
    spread = hits.T.astype(BF16)
    spread = jnp.concatenate([spread, spread], axis=1)

    loads[2].wait()
    loads[3].wait()
    links, laws = [], []
    for v in range(OWN):
        element = OWN * spoke + v
        own_row = lax.broadcasted_iota(jnp.int32, (TILES, LINKS), 0) == element
        links.append(jnp.sum(jnp.where(own_row, pattern, 0), axis=0, keepdims=True))
        region = reg[...].reshape(1, TILES)
        lane = lax.broadcasted_iota(jnp.int32, (1, TILES), 1)
        region = jnp.sum(jnp.where(lane == element, region, 0), axis=1, keepdims=True)
        lane = lax.broadcasted_iota(jnp.int32, (3, 4), 1)
        own_law = jnp.sum(jnp.where(lane == region, law[...], 0.0), axis=1, keepdims=True)
        laws.append((own_law[0:1], own_law[1:2], own_law[2:3]))

    @pl.when(is_hub)
    def _():
        loads[4].wait()
        loads[5].wait()

    def remote(src, dst, i, group, other):
        return pltpu.make_async_remote_copy(
            src_ref=src, dst_ref=dst, send_sem=send_sem.at[i], recv_sem=recv_sem.at[i],
            device_id=at(group, other), device_id_type=MESH,
        )

    pl.semaphore_wait(barrier, jnp.where(is_hub, 2 * HUBS - 1, 2 * HUBS))

    @pl.when(is_hub)
    def _():
        pl.semaphore_signal(
            ready, inc=1, device_id=at(after, jnp.where(rank == 0, 4, rank)), device_id_type=MESH
        )

    first, last = coef.at[:, pl.ds(0, TILE)], coef.at[:, pl.ds((TILES - 1) * TILE, TILE)]
    sent_first = [remote(first, firsts.at[rank], 0, space, other) for other in hubs]
    sent_last = [remote(last, low_got.at[rank], 1, after, other) for other in [home, *hubs]]
    sent_picks = [
        remote(picks.at[u], got.at[rank], 3, space, hub_rank(u)) for u in others_spokes
    ]
    home_first = remote(first, firsts.at[rank], 0, space, home)
    home_picks = remote(picks.at[spoke], got.at[rank], 3, space, home)

    @pl.when(jnp.logical_not(is_hub))
    def _():
        home_first.start()

    for copy in sent_first + sent_last:
        copy.start()

    @pl.when(jnp.logical_not(is_hub))
    def _():
        home_picks.start()

    for copy in sent_picks:
        copy.start()

    def block(ref, which):
        start = which * ROWS if isinstance(which, int) else pl.multiple_of(which * ROWS, ROWS)
        return ref.at[pl.ds(start, ROWS)]

    @pl.when(is_hub)
    def _():
        firsts[rank] = coef[:, 0:TILE]
        got[rank] = picks[spoke]
        for v in range(OWN):
            curl_t[v] = curl[v].reshape(LINKS * TILE, COMP).T
        gathered = firsts.at[pl.ds(0, GROUP - 1)]
        remote(gathered, gathered, 0, space, hubs[0]).wait_recv()
        handed = remote(firsts, high_got, 2, before, rank)

        @pl.when(rank != 0)
        def _():
            pl.semaphore_wait(ready, jnp.where(rank == 4, 2, 1))
            handed.start()

        @pl.when(rank == 4)
        def _():
            remote(firsts, high_got, 2, before, 0).start()

        picked = got.at[pl.ds(0, GROUP - 1)]
        remote(picked, picked, 3, space, hubs[0]).wait_recv()
        windows = jnp.concatenate(
            [got[:, v].reshape(GROUP * EDGE, TILE) for v in range(OWN)], axis=1
        )
        waves = jnp.dot(
            tab[0:WAVES, :],
            jnp.concatenate([windows, windows], axis=0),
            preferred_element_type=F32,
        )
        remote(low_got, low_got, 1, space, hubs[0]).wait_recv()
        halo = [low_got[...].astype(F32).reshape(PARTS, TILE).astype(BF16)]
        handed.wait_recv()
        halo.append(high_got[...].astype(F32).reshape(PARTS, TILE).astype(BF16))
        halo = jnp.dot(
            tab[WAVES : WAVES + 2 * HALF, 0:TILE],
            jnp.concatenate([*halo, *halo], axis=0),
            preferred_element_type=F32,
        )
        halo = [halo[:HALF], halo[HALF:]]
        back = tab[WAVES + 2 * HALF : WAVES + 2 * HALF + PARTS, 0 : 3 * HALF]
        edges = [jnp.zeros((PARTS, TILE), F32), jnp.zeros((PARTS, TILE), F32)]
        densities = []
        for v in range(OWN):
            wave = []
            for k in range(LINKS):
                piece = waves[k * HALF : (k + 1) * HALF, v * TILE : (v + 1) * TILE]
                for i, spot in enumerate((0, TILES + 1)):
                    piece = piece + jnp.where(links[v][:, k : k + 1] == spot, halo[i], 0.0)
                wave.append(piece)
            densities.append(
                jnp.dot(
                    jnp.concatenate(split(jnp.concatenate(wave, axis=1)), axis=0),
                    curl[v].reshape(LINKS * TILE, COMP),
                    preferred_element_type=F32,
                )
            )
        fields = []
        for v in range(OWN):
            density = densities[v][:HALF] + densities[v][HALF:]
            comps = [density[:, c * TILE : (c + 1) * TILE] for c in range(3)]
            square = comps[0] * comps[0] + comps[1] * comps[1] + comps[2] * comps[2]
            base, knee, rise = laws[v]
            reluct = base + rise * square / (square + knee)
            high, low = split(jnp.concatenate([reluct * c for c in comps], axis=1))
            fields.append(jnp.concatenate([high, high, low], axis=0))
        harmonics = [jnp.dot(back, f, preferred_element_type=F32).astype(BF16) for f in fields]
        contribs = [
            jnp.dot(harmonics[v], curl_t[v], preferred_element_type=F32) for v in range(OWN)
        ]
        for v in range(OWN):
            for k in range(LINKS):
                tile = contribs[v][:, k * TILE : (k + 1) * TILE]
                for i, spot in enumerate((0, TILES + 1)):
                    edges[i] = edges[i] + jnp.where(links[v][:, k : k + 1] == spot, tile, 0.0)
        for i in range(2):
            for p in range(2):
                edge_flow[i, :, p, :] = edges[i][p * GROUP : (p + 1) * GROUP]

        to_after = [remote(edge_flow.at[1, o], low_flow.at[spoke], 4, after, o) for o in launched]
        to_before = [remote(edge_flow.at[0, o], high_flow.at[spoke], 5, before, o) for o in launched]
        to_group = [remote(block(flow, o), block(flow_got, spoke), 6, space, o) for o in launched]
        for copy in to_after:
            copy.start()
        for v in range(OWN):
            for k in range(LINKS):
                for p in range(2):
                    flow[pl.ds(v * EDGE + 2 * k + p, GROUP, stride=ROWS), :] = contribs[v][
                        p * GROUP : (p + 1) * GROUP, k * TILE : (k + 1) * TILE
                    ]
        for other, *copies in zip(launched, to_group, to_before):

            @pl.when(rank != other)
            def _():
                copies[0].start()

            copies[1].start()
        mine = pl.ds(pl.multiple_of(spoke * ROWS, ROWS), ROWS)
        flow_got[mine, :] = flow[pl.ds(pl.multiple_of(rank * ROWS, ROWS), ROWS), :]
        others = pl.ds(0, (HUBS - 1) * ROWS)
        remote(flow_got.at[others], flow_got.at[others], 6, space, hubs[0]).wait_recv()

    @pl.when(jnp.logical_not(is_hub))
    def _():
        remote(flow_got, flow_got, 6, space, home).wait_recv()

    owned = jnp.dot(
        spread, jnp.concatenate(split(flow_got[...]), axis=0), preferred_element_type=F32
    )
    for w in range(1, TILES - 1):
        out_ref[:, w * TILE : (w + 1) * TILE] = owned[2 * w : 2 * w + 2]
    for copy in sent_first + sent_last + sent_picks:
        copy.wait_send()

    @pl.when(jnp.logical_not(is_hub))
    def _():
        home_first.wait_send()
        home_picks.wait_send()

    @pl.when(is_hub)
    def _():
        others = pl.ds(0, (GROUP - 1) * ROWS)

        @pl.when(rank != 0)
        def _():
            remote(firsts, high_got, 2, before, rank).wait_send()

        @pl.when(rank == 4)
        def _():
            remote(firsts, high_got, 2, before, 0).wait_send()

        remote(edge_flow.at[1], edge_flow.at[1], 4, after, home).wait_send()
        remote(edge_flow.at[0], edge_flow.at[0], 5, after, home).wait_send()
        remote(flow.at[others], flow.at[others], 6, after, home).wait_send()

    for w, edge, i in ((TILES - 1, high_flow, 5), (0, low_flow, 4)):
        remote(edge, edge, i, after, home).wait_recv()
        edge_sum = (edge[0] + edge[1]) + (edge[2] + edge[3])
        out_ref[:, w * TILE : (w + 1) * TILE] = owned[2 * w : 2 * w + 2] + edge_sum


def per_device(coeffs, curl_tiles, pattern, region_ids, material_law, source):
    anywhere = pl.BlockSpec(memory_space=pltpu.HBM)
    table = tables()
    total = pl.pallas_call(
        kernel,
        out_shape=pltpu.VMEM(source.shape, F32),
        in_specs=[anywhere] * 6,
        out_specs=pl.BlockSpec(memory_space=pltpu.VMEM),
        scratch_shapes=[
            pltpu.VMEM((2, TILES * TILE), BF16),
            pltpu.VMEM((OWN, LINKS, TILE, COMP), BF16),
            pltpu.VMEM((LINKS, TILES), jnp.int32),
            pltpu.VMEM((TILES,), jnp.int32),
            pltpu.VMEM((3, 4), F32),
            pltpu.VMEM(table.shape, BF16),
            pltpu.VMEM((HUBS, OWN, EDGE, TILE), BF16),
            pltpu.VMEM((GROUP, OWN, EDGE, TILE), BF16),
            pltpu.VMEM((GROUP, 2, TILE), BF16),
            pltpu.VMEM((GROUP, 2, TILE), BF16),
            pltpu.VMEM((GROUP, 2, TILE), BF16),
            pltpu.VMEM((GROUP * ROWS, TILE), F32),
            pltpu.VMEM((HUBS * ROWS, TILE), F32),
            pltpu.VMEM((2, GROUP, 2, TILE), F32),
            pltpu.VMEM((HUBS, 2, TILE), F32),
            pltpu.VMEM((HUBS, 2, TILE), F32),
            pltpu.SemaphoreType.DMA((6,)),
            pltpu.SemaphoreType.DMA((7,)),
            pltpu.SemaphoreType.DMA((7,)),
            pltpu.SemaphoreType.REGULAR,
            pltpu.VMEM((OWN, COMP, LINKS * TILE), BF16),
        ],
        compiler_params=pltpu.CompilerParams(collective_id=0, has_side_effects=True),
        name="residual",
    )(coeffs, curl_tiles, pattern.T, region_ids, material_law, jnp.asarray(table))
    return total - source


def solution(mesh):
    placed = (
        P(("harm", "samp"), "space"),
        P("space", None, None, None),
        P("space", None),
        P("space"),
        P(),
        P(("harm", "samp"), "space"),
    )
    return jax.shard_map(
        per_device,
        mesh=mesh,
        in_specs=placed,
        out_specs=P(("harm", "samp"), "space"),
        check_vma=False,
    )
```
